32 devices in a mesh: freq: 2 (over y), clus: 4 (over z), rows: 4 (over x, core).
Axes of the slice: x: 2, y: 2, z: 4, core: 2. Of those that a mesh axis runs over, the one named last changes fastest.
Arguments:
- excitation: bfloat16 [8192, 2, 128], P(('freq', 'clus', 'rows')), parts along dimension 0, may hold values from -6 to 6
- leaf_factor: bfloat16 [4, 4, 4, 32, 1024], P('freq', 'clus', None, 'rows'), parts along dimension 0, may hold values from -0.125 to 0.125
- coupling: bfloat16 [4, 4, 4, 32, 1024], P('freq', 'clus', None, 'rows'), parts along dimension 0, may hold values from -0.375 to 0.375
- ranks: int32 [8, 4], P('freq'), parts along dimension 0, may hold values from 8 to 32, as said below
Outputs:
- field: bfloat16 [8192, 2, 128], P(('freq', 'clus', 'rows')), parts along dimension 0
The draws below stay inside these ranges and needn't reach their ends.
There are 2 independent parts, one for each index of `freq`. The reference program is written for one: setup_inputs(seed, part) draws one part's arguments, and reference() takes and returns one part's arrays. A program takes and returns all parts, laid end to end along the dimension named above; each array names one. Nothing has to cross between parts.
Inputs may be any that keep to these rules, and one draw needn't show every extreme that they name: `ranks`: each block's rank.
All inputs are finite; a program needn't handle non-finite values.
Results may differ from the reference program's by a relative error of at most 0.0076.
Values may be sent and summed in bfloat16 or wider, within the bound.
No kernel may reach another device: no remote copies, remote signals or barrier semaphores. Data moves between devices by JAX's collectives and lax.ppermute only.
A program may use at most 64 MiB of HBM per device.

```python
import jax
import jax.numpy as jnp
from jax import lax

M = 1024
R = 128
Q = 32
STEPS = 3
C = 4
N = 4096


def draw_ranks(key, part):
    key = jax.random.fold_in(key, 7)
    base = jax.random.randint(key, (C, C), Q // 4, Q + 1, dtype=jnp.int32)
    row_index = jnp.arange(C, dtype=jnp.int32)[:, None]
    col_index = jnp.arange(C, dtype=jnp.int32)[None, :]
    base = jnp.where(row_index == col_index, Q, base)
    base = jnp.where(col_index == (row_index + 1) % C, Q // 4, base)
    return base.astype(jnp.int32)


def block_levels(rng, shape, shards, least, high):
    level = 1.0
    for axis_at, shards_of in shards:
        steps = jax.random.uniform(jax.random.fold_in(jax.random.fold_in(rng, 6), axis_at), (shards_of,), jnp.float32, least / len(shards), high / len(shards))
        level = level * jnp.repeat(jnp.exp(steps), shape[axis_at] // shards_of).reshape((-1,) + (1,) * (len(shape) - 1 - axis_at))
    return level


def bell_draw(key, extent, deviation, bound, cuts=(), held_as=jnp.bfloat16):
    values = deviation * jax.random.normal(key, extent, jnp.float32)
    if cuts:
        values = values * block_levels(key, extent, cuts, -0.22, 0.18)
    return jnp.clip(values, -bound, bound).astype(held_as)


def setup_inputs(seed: int = 0, part: int = 0) -> dict:
    arg_keys = jax.random.split(jax.random.key(seed), 5)
    own_keys = jax.random.split(jax.random.fold_in(arg_keys[4], part), 5)
    excitation = bell_draw(own_keys[0], (N, 2, R), 1.0, 6.0, ((0, 16),))
    leaf_factor = bell_draw(own_keys[1], (2, C, C, Q, M), (2 * M) ** -0.5, 0.125, ((1, 4), (3, 4)))
    coupling = bell_draw(own_keys[2], (2, C, C, Q, M), (2 * C * Q) ** -0.5, 0.375, ((1, 4), (3, 4)))
    ranks = draw_ranks(jax.random.fold_in(jax.random.fold_in(arg_keys[4], part), 71), part)
    return dict(excitation=excitation, leaf_factor=leaf_factor, coupling=coupling, ranks=ranks)


def complex_dot(a_real, a_imag, b_real, b_imag):
    real_part = jnp.dot(a_real, b_real, preferred_element_type=jnp.float32) - jnp.dot(a_imag, b_imag, preferred_element_type=jnp.float32)
    imag_part = jnp.dot(a_real, b_imag, preferred_element_type=jnp.float32) + jnp.dot(a_imag, b_real, preferred_element_type=jnp.float32)
    return real_part, imag_part


def apply_once(current, leaf_factor, coupling, ranks):
    angles_all = current.reshape(C, M, 2, R)

    def leaf_level(source):
        factor = lax.dynamic_index_in_dim(leaf_factor, source, 1, keepdims=False).reshape(2, C * Q, M)
        local = lax.dynamic_index_in_dim(angles_all, source, 0, keepdims=False)
        real_part, imag_part = complex_dot(factor[0], factor[1], local[:, 0], local[:, 1])
        return jnp.stack([real_part, imag_part]).astype(jnp.bfloat16).reshape(2, C, Q, R)

    skeleton = lax.map(leaf_level, jnp.arange(C, dtype=jnp.int32))
    rank_level = jnp.arange(Q, dtype=jnp.int32)

    def target_level(target):
        factor = lax.dynamic_index_in_dim(coupling, target, 1, keepdims=False).reshape(2, C * Q, M)
        received = lax.dynamic_index_in_dim(skeleton, target, 2, keepdims=False)
        rank_row = lax.dynamic_index_in_dim(ranks, target, 0, keepdims=False)
        keep_mask = (rank_level[None, :] < rank_row[:, None]).astype(received.dtype)
        received = received * keep_mask[:, None, :, None]
        received = jnp.transpose(received, (1, 0, 2, 3)).reshape(2, C * Q, R)
        real_part, imag_part = complex_dot(factor[0].T, factor[1].T, received[0], received[1])
        return jnp.stack([real_part, imag_part], axis=1).astype(jnp.bfloat16)

    field = lax.map(target_level, jnp.arange(C, dtype=jnp.int32))
    return field.reshape(C * M, 2, R)


def reference(excitation, leaf_factor, coupling, ranks):
    current = excitation
    for step in range(STEPS):
        current = apply_once(current, leaf_factor, coupling, ranks)
    return current
```

```python
import functools

import jax
import jax.numpy as jnp
from jax import lax
from jax.experimental import pallas as pl
from jax.experimental.pallas import tpu as pltpu
from jax.sharding import PartitionSpec as P

STEPS = 3
F32 = jnp.float32
BF16 = jnp.bfloat16
SMALL_GATHER = 4 << 20


def complex_dot(a_real, a_imag, b_real, b_imag):
    real_part = jnp.dot(a_real, b_real, preferred_element_type=F32) - jnp.dot(
        a_imag, b_imag, preferred_element_type=F32
    )
    imag_part = jnp.dot(a_real, b_imag, preferred_element_type=F32) + jnp.dot(
        a_imag, b_real, preferred_element_type=F32
    )
    return (real_part, imag_part)


def transposed_dot(columns, skel_flat):
    real_part = jnp.einsum(
        "km,kr->mr", columns[0], skel_flat[0], preferred_element_type=F32
    ) - jnp.einsum("km,kr->mr", columns[1], skel_flat[1], preferred_element_type=F32)
    imag_part = jnp.einsum(
        "km,kr->mr", columns[0], skel_flat[1], preferred_element_type=F32
    ) + jnp.einsum("km,kr->mr", columns[1], skel_flat[0], preferred_element_type=F32)
    return jnp.stack([real_part, imag_part], axis=1)


def apply_once(current, factor, weights, keep_mask, clusters, quarter, leaf_size, angles, part_row):
    gathered = lax.all_gather(current, "rows", axis=0, tiled=True)
    real_part, imag_part = complex_dot(factor[0], factor[1], gathered[:, 0], gathered[:, 1])
    skeleton = jnp.stack([real_part, imag_part]).astype(BF16).reshape(2, clusters, quarter, angles)
    received = lax.all_to_all(skeleton, "clus", split_axis=1, concat_axis=1, tiled=True)
    received = received * keep_mask[None, :, :, None]
    skel_flat = received.reshape(2, clusters * quarter, angles)
    share_rows = leaf_size // lax.axis_size("rows")
    partial_sum = transposed_dot(weights, skel_flat)
    summed = lax.psum(partial_sum, "rows")
    own_rows = lax.dynamic_slice_in_dim(summed, part_row * share_rows, share_rows, 0)
    return own_rows.astype(BF16)


def step_body(excitation, leaf_factor, coupling, ranks):
    cluster = lax.axis_index("clus")
    part_row = lax.axis_index("rows")
    clusters = leaf_factor.shape[2]
    quarter = leaf_factor.shape[3]
    leaf_size = leaf_factor.shape[4]
    angles = excitation.shape[2]
    factor = leaf_factor.reshape(2, clusters * quarter, leaf_size)
    weights = coupling.reshape(2, clusters * quarter, leaf_size)
    rank_row = lax.dynamic_slice_in_dim(ranks, cluster, 1, 0)[0]
    rank_level = part_row * quarter + jnp.arange(quarter, dtype=jnp.int32)
    keep_mask = (rank_level[None, :] < rank_row[:, None]).astype(BF16)
    current = excitation
    for step in range(STEPS):
        current = apply_once(
            current, factor, weights, keep_mask, clusters, quarter, leaf_size, angles, part_row
        )
    return current


def aligned(index, step):
    return pl.multiple_of(index, step)


def rows_of(block):
    flat = block.astype(F32).reshape(block.shape[0] * block.shape[1], block.shape[2])
    return flat.astype(BF16)


def combine(product, rows, columns):
    real_part = product[:rows, :columns] - product[rows:, columns:]
    imag_part = product[:rows, columns:] + product[rows:, :columns]
    return real_part, imag_part


def local_kernel(
    clusters, quarter, leaf, share, angles,
    ranks, l_own, l_x, k_own, k_x, k_core, k_diag, x_own, x_x, x_core, x_diag,
    packed, k_mine, l_all, k_all, x_all, x_wide,
):
    row = lax.axis_index("rows")
    cluster = lax.axis_index("clus")
    side, core = row // 2, row % 2
    block = clusters * quarter
    full = 4 * block
    for ref, at in ((l_own, side), (l_x, 1 - side)):
        for part in range(2):
            l_all[pl.ds(aligned(part * 2 * block + at * block, block), block), :] = rows_of(ref[part])
    for ref, at in ((k_own, row), (k_x, row ^ 2), (k_core, row ^ 1), (k_diag, row ^ 3)):
        for part in range(2):
            k_all[pl.ds(aligned(part * full + at * block, block), block), :] = rows_of(ref[part])
    for ref, at in ((x_own, row), (x_x, row ^ 2), (x_core, row ^ 1), (x_diag, row ^ 3)):
        x_wide[...] = ref[...].astype(F32)
        own_rows = pl.ds(aligned(at * share, share), share)
        for part in range(2):
            x_all[own_rows, part * angles : (part + 1) * angles] = x_wide[
                pl.ds(part, share, stride=2), :
            ].astype(BF16)
    skeleton = jnp.dot(l_all[...], x_all[...], preferred_element_type=F32)
    between = lax.dot_general(
        l_all[...], k_all[...], (((1,), (1,)), ((), ())), preferred_element_type=F32
    )
    parts = combine(skeleton, 2 * block, angles) + combine(between, 2 * block, full)
    level = lax.broadcasted_iota(jnp.int32, (quarter, 128), 0)
    for at in range(2):
        base = (2 * at + core) * quarter
        kept = [level + base < ranks[target, cluster] for target in range(clusters)]
        for i, value in enumerate(parts):
            rows = [
                jnp.where(
                    kept[target],
                    value[at * block + target * quarter : at * block + (target + 1) * quarter],
                    0.0,
                )
                for target in range(clusters)
            ]
            packed[at, i] = jnp.concatenate(rows, axis=0).astype(BF16)
    for part in range(2):
        k_mine[part] = k_all[part * full : (part + 1) * full, pl.ds(aligned(row * share, share), share)]


def chain_kernel(clusters, quarter, share, angles, *refs):
    held, swapped = refs[:clusters], refs[clusters : 2 * clusters]
    k_mine, field, between, skeleton, kept, wide = refs[2 * clusters :]
    row = lax.axis_index("rows")
    cluster = lax.axis_index("clus")
    core = row % 2
    block = clusters * quarter
    full = 4 * block
    for j in range(clusters):
        source = cluster ^ j
        for ref, at_core in ((held[j], core), (swapped[j], 1 - core)):
            for at in range(2):
                first = (2 * at + at_core) * block
                for part in range(2):
                    skeleton[source, part, pl.ds(aligned(first, block), block), :] = ref[
                        at, part
                    ].astype(F32)
                    between[source, pl.ds(aligned(part * full + first, block), block), :] = ref[
                        at, 2 + part
                    ]

    def regroup(target):
        columns = []
        for part in range(2):
            rows = [
                skeleton[s, part, pl.ds(aligned(q * block + target * quarter, quarter), quarter), :]
                for q in range(4)
                for s in range(clusters)
            ]
            columns.append(jnp.concatenate(rows, axis=0))
        return jnp.concatenate(columns, axis=1).astype(BF16)

    for step in range(STEPS - 1):
        for target in range(clusters):
            kept[target] = regroup(target)
        for source in range(clusters):
            product = jnp.dot(between[source], kept[source], preferred_element_type=F32)
            skeleton[source, 0], skeleton[source, 1] = combine(product, full, angles)
    last = regroup(cluster)
    contract = (((0,), (0,)), ((), ()))
    with_real = lax.dot_general(k_mine[0], last, contract, preferred_element_type=F32)
    with_imag = lax.dot_general(k_mine[1], last, contract, preferred_element_type=F32)
    wide[pl.ds(0, share, stride=2), :] = with_real[:, :angles] - with_imag[:, angles:]
    wide[pl.ds(1, share, stride=2), :] = with_real[:, angles:] + with_imag[:, :angles]
    field[...] = wide[...].astype(BF16)


def in_vmem(count):
    return [pl.BlockSpec(memory_space=pltpu.VMEM)] * count


def gather_body(excitation, leaf_factor, coupling, ranks):
    clusters, quarter, leaf = leaf_factor.shape[2:]
    share, _, angles = excitation.shape
    block = clusters * quarter
    full = 4 * block

    def across(flip):
        return lambda v: lax.ppermute(v, "rows", [(i, i ^ flip) for i in range(4)])

    to_x, to_core = across(2), across(1)
    own_x = excitation.reshape(2 * share, angles)
    own_l = leaf_factor.reshape(2, clusters, quarter, leaf)
    own_k = coupling.reshape(2, clusters, quarter, leaf)
    l_x, k_x, x_x = to_x(own_l), to_x(own_k), to_x(own_x)
    k_core, x_core = to_core(own_k), to_core(own_x)
    k_diag, x_diag = to_core(k_x), to_core(x_x)
    packed, k_mine = pl.pallas_call(
        functools.partial(local_kernel, clusters, quarter, leaf, share, angles),
        out_shape=(
            jax.ShapeDtypeStruct((2, 4, block, angles), BF16),
            jax.ShapeDtypeStruct((2, full, share), BF16),
        ),
        in_specs=[pl.BlockSpec(memory_space=pltpu.SMEM)] + in_vmem(10),
        out_specs=tuple(in_vmem(2)),
        scratch_shapes=[
            pltpu.VMEM((4 * block, leaf), BF16),
            pltpu.VMEM((2 * full, leaf), BF16),
            pltpu.VMEM((leaf, 2 * angles), BF16),
            pltpu.VMEM((2 * share, angles), F32),
        ],
        compiler_params=pltpu.CompilerParams(vmem_limit_bytes=32 << 20),
        name="local_skeleton",
    )(ranks, own_l, l_x, own_k, k_x, k_core, k_diag, own_x, x_x, x_core, x_diag)
    held = [packed] + [
        lax.ppermute(packed, "clus", [(i, i ^ j) for i in range(clusters)])
        for j in range(1, clusters)
    ]
    swapped = [to_core(v) for v in held]
    field = pl.pallas_call(
        functools.partial(chain_kernel, clusters, quarter, share, angles),
        out_shape=jax.ShapeDtypeStruct((2 * share, angles), BF16),
        in_specs=in_vmem(2 * clusters + 1),
        out_specs=in_vmem(1)[0],
        scratch_shapes=[
            pltpu.VMEM((clusters, 2 * full, full), BF16),
            pltpu.VMEM((clusters, 2, full, angles), F32),
            pltpu.VMEM((clusters, full, 2 * angles), BF16),
            pltpu.VMEM((2 * share, angles), F32),
        ],
        compiler_params=pltpu.CompilerParams(vmem_limit_bytes=32 << 20),
        name="skeleton_chain",
    )(*held, *swapped, k_mine)
    return field.reshape(share, 2, angles)


def body(excitation, leaf_factor, coupling, ranks):
    clusters, quarter, leaf = leaf_factor.shape[2:]
    share, _, angles = excitation.shape
    rows = lax.axis_size("rows")
    full = rows * clusters * quarter
    gathered = 4 * clusters * full * (angles + full)
    fits = (
        rows == 4
        and clusters == lax.axis_size("clus")
        and clusters & (clusters - 1) == 0
        and quarter == 8
        and angles == full == 128
        and share * rows == leaf
        and gathered <= SMALL_GATHER
    )
    plan = gather_body if fits else step_body
    return plan(excitation, leaf_factor, coupling, ranks)


def solution(mesh):
    placed = (
        P(("freq", "clus", "rows"), None, None),
        P("freq", "clus", None, "rows", None),
        P("freq", "clus", None, "rows", None),
        P("freq", None),
    )
    return jax.shard_map(
        body,
        mesh=mesh,
        in_specs=placed,
        out_specs=P(("freq", "clus", "rows"), None, None),
        check_vma=False,
    )
```

```python
import functools

import jax
import jax.numpy as jnp
from jax import lax
from jax.experimental import pallas as pl
from jax.experimental.pallas import tpu as pltpu
from jax.sharding import PartitionSpec as P

STEPS = 3
F32 = jnp.float32
BF16 = jnp.bfloat16
SMALL_GATHER = 4 << 20


def complex_dot(a_real, a_imag, b_real, b_imag):
    real_part = jnp.dot(a_real, b_real, preferred_element_type=F32) - jnp.dot(
        a_imag, b_imag, preferred_element_type=F32
    )
    imag_part = jnp.dot(a_real, b_imag, preferred_element_type=F32) + jnp.dot(
        a_imag, b_real, preferred_element_type=F32
    )
    return (real_part, imag_part)


def transposed_dot(columns, skel_flat):
    real_part = jnp.einsum(
        "km,kr->mr", columns[0], skel_flat[0], preferred_element_type=F32
    ) - jnp.einsum("km,kr->mr", columns[1], skel_flat[1], preferred_element_type=F32)
    imag_part = jnp.einsum(
        "km,kr->mr", columns[0], skel_flat[1], preferred_element_type=F32
    ) + jnp.einsum("km,kr->mr", columns[1], skel_flat[0], preferred_element_type=F32)
    return jnp.stack([real_part, imag_part], axis=1)


def apply_once(current, factor, weights, keep_mask, clusters, quarter, leaf_size, angles, part_row):
    gathered = lax.all_gather(current, "rows", axis=0, tiled=True)
    real_part, imag_part = complex_dot(factor[0], factor[1], gathered[:, 0], gathered[:, 1])
    skeleton = jnp.stack([real_part, imag_part]).astype(BF16).reshape(2, clusters, quarter, angles)
    received = lax.all_to_all(skeleton, "clus", split_axis=1, concat_axis=1, tiled=True)
    received = received * keep_mask[None, :, :, None]
    skel_flat = received.reshape(2, clusters * quarter, angles)
    share_rows = leaf_size // lax.axis_size("rows")
    partial_sum = transposed_dot(weights, skel_flat)
    summed = lax.psum(partial_sum, "rows")
    own_rows = lax.dynamic_slice_in_dim(summed, part_row * share_rows, share_rows, 0)
    return own_rows.astype(BF16)


def step_body(excitation, leaf_factor, coupling, ranks):
    cluster = lax.axis_index("clus")
    part_row = lax.axis_index("rows")
    clusters = leaf_factor.shape[2]
    quarter = leaf_factor.shape[3]
    leaf_size = leaf_factor.shape[4]
    angles = excitation.shape[2]
    factor = leaf_factor.reshape(2, clusters * quarter, leaf_size)
    weights = coupling.reshape(2, clusters * quarter, leaf_size)
    rank_row = lax.dynamic_slice_in_dim(ranks, cluster, 1, 0)[0]
    rank_level = part_row * quarter + jnp.arange(quarter, dtype=jnp.int32)
    keep_mask = (rank_level[None, :] < rank_row[:, None]).astype(BF16)
    current = excitation
    for step in range(STEPS):
        current = apply_once(
            current, factor, weights, keep_mask, clusters, quarter, leaf_size, angles, part_row
        )
    return current


def combine(product, rows, columns):
    real_part = product[:rows, :columns] - product[rows:, columns:]
    imag_part = product[:rows, columns:] + product[rows:, :columns]
    return real_part, imag_part


def load_kernel(
    share, angles, quarter, ranks, l_hbm, k_hbm, x_hbm, x_near,
    l_own, k_own, x_own, x_core, keep, x_flat, x_wide, sems,
):
    copies = [
        pltpu.make_async_copy(source, target, sems.at[i])
        for i, (source, target) in enumerate(((x_hbm, x_flat), (l_hbm, l_own), (k_hbm, k_own)))
    ]
    for copy in copies:
        copy.start()
    row = lax.axis_index("rows")
    cluster = lax.axis_index("clus")
    level = lax.broadcasted_iota(jnp.int32, (quarter, angles), 0)
    for at, flip in enumerate((0, 2, 1, 3)):
        base = (row ^ flip) * quarter
        for target in range(keep.shape[1] // quarter):
            below = level + base < ranks[target, cluster]
            keep[at, target * quarter : (target + 1) * quarter, :] = below.astype(F32)
    copies[0].wait()
    for source, target in ((x_flat, x_own), (x_near, x_core)):
        x_wide[...] = source[...].astype(F32)
        for part in range(2):
            target[:, part * angles : (part + 1) * angles] = x_wide[
                pl.ds(part, share, stride=2), :
            ].astype(BF16)
    copies[1].wait()
    copies[2].wait()


def side_kernel(share, angles, l_own, l_x, x_own, x_core, partial, kept_partial, l_all):
    row = lax.axis_index("rows")
    block = l_own.shape[1]
    for part in range(2):
        for at, ref in enumerate((l_own, l_x)):
            first = (2 * part + at) * block
            l_all[first : first + block, :] = ref[part]
    total = None
    for ref, quarter in ((x_own, row), (x_core, row ^ 1)):
        columns = l_all[:, pl.ds(pl.multiple_of(quarter * share, share), share)]
        term = jnp.dot(columns, ref[...], preferred_element_type=F32)
        total = term if total is None else total + term
    for part, value in enumerate(combine(total, 2 * block, angles)):
        for at in range(2):
            rows = value[at * block : (at + 1) * block]
            kept_partial[at, part] = rows
            partial[at, part] = rows.astype(BF16)


def operator_columns(l_all, k_refs, k_rows):
    block = k_refs[0].shape[1]
    for part in range(2):
        for at, ref in enumerate(k_refs):
            first = (2 * part + at) * block
            k_rows[first : first + block, :] = ref[part]
    product = lax.dot_general(
        l_all[...], k_rows[...], (((1,), (1,)), ((), ())), preferred_element_type=F32
    )
    return combine(product, 2 * block, 2 * block)


def near_kernel(l_all, k_own, k_core, near, k_rows):
    near[0], near[1] = operator_columns(l_all, (k_own, k_core), k_rows)


def between_kernel(partial, partial_x, near, keep, l_all, k_x, k_diag, packed, k_rows):
    block = keep.shape[1]
    parts = []
    for part, far in enumerate(operator_columns(l_all, (k_x, k_diag), k_rows)):
        value = near[part]
        columns = [value[:, :block], far[:, :block], value[:, block:], far[:, block:]]
        parts.append(jnp.concatenate(columns, axis=1))
    for at in range(2):
        values = [partial[at, part] + partial_x[1 - at, part].astype(F32) for part in range(2)]
        values += [value[at * block : (at + 1) * block] for value in parts]
        for i, value in enumerate(values):
            packed[at, i] = (value * keep[at]).astype(BF16)


def chain_kernel(clusters, quarter, share, angles, *refs):
    pieces, k_quarters = refs[: 2 * clusters], refs[2 * clusters : 2 * clusters + 4]
    field, between, skeleton, kept, wide, k_mine = refs[2 * clusters + 4 :]
    row = lax.axis_index("rows")
    cluster = lax.axis_index("clus")
    block = clusters * quarter
    full = 4 * block
    for at in range(4):
        for part in range(2):
            k_mine[part, at * block : (at + 1) * block, :] = k_quarters[at][
                part, :, pl.ds(pl.multiple_of(row * share, share), share)
            ]
    for j in range(clusters):
        source = cluster ^ j
        for core in range(2):
            ref = pieces[2 * j + core]
            for at in range(2):
                first = (2 * core + at) * block
                for part in range(2):
                    skeleton[source, part, first : first + block, :] = ref[at, part].astype(F32)
                    value = ref[at, 2 + part]
                    if core:
                        value = pltpu.roll(value.astype(F32), full // 2, 1).astype(BF16)
                    between[source, part * full + first : part * full + first + block, :] = value

    def regroup(target):
        columns = []
        for part in range(2):
            rows = [
                skeleton[s, part, pl.ds(pl.multiple_of(q * block + target * quarter, quarter), quarter), :]
                for q in range(4)
                for s in range(clusters)
            ]
            columns.append(jnp.concatenate(rows, axis=0))
        return jnp.concatenate(columns, axis=1).astype(BF16)

    for step in range(STEPS - 1):
        for target in range(clusters):
            kept[target] = regroup(target)
        for source in range(clusters):
            product = jnp.dot(between[source], kept[source], preferred_element_type=F32)
            skeleton[source, 0], skeleton[source, 1] = combine(product, full, angles)
    last = regroup(cluster)
    contract = (((0,), (0,)), ((), ()))
    with_real = lax.dot_general(k_mine[0], last, contract, preferred_element_type=F32)
    with_imag = lax.dot_general(k_mine[1], last, contract, preferred_element_type=F32)
    wide[pl.ds(0, share, stride=2), :] = with_real[:, :angles] - with_imag[:, angles:]
    wide[pl.ds(1, share, stride=2), :] = with_real[:, angles:] + with_imag[:, :angles]
    field[...] = wide[...].astype(BF16)


def in_vmem(count):
    return [pl.BlockSpec(memory_space=pltpu.VMEM)] * count


def gather_body(excitation, leaf_factor, coupling, ranks):
    clusters, quarter, leaf = leaf_factor.shape[2:]
    share, _, angles = excitation.shape
    block = clusters * quarter
    full = 4 * block
    params = pltpu.CompilerParams(vmem_limit_bytes=32 << 20)

    def across(flip):
        return lambda v: lax.ppermute(v, "rows", [(i, i ^ flip) for i in range(4)])

    to_x, to_core = across(2), across(1)
    factor = leaf_factor.reshape(2, block, leaf)
    weights = coupling.reshape(2, block, leaf)
    l_x, k_x = to_x(factor), to_x(weights)
    current = excitation.reshape(2 * share, angles)
    x_near = to_core(current)
    k_core = to_core(weights)
    l_own, k_own, x_own, x_core, keep = pl.pallas_call(
        functools.partial(load_kernel, share, angles, quarter),
        out_shape=(
            jax.ShapeDtypeStruct(factor.shape, BF16),
            jax.ShapeDtypeStruct(weights.shape, BF16),
            jax.ShapeDtypeStruct((share, 2 * angles), BF16),
            jax.ShapeDtypeStruct((share, 2 * angles), BF16),
            jax.ShapeDtypeStruct((4, block, angles), F32),
        ),
        in_specs=[pl.BlockSpec(memory_space=pltpu.SMEM)]
        + [pl.BlockSpec(memory_space=pl.ANY)] * 3
        + in_vmem(1),
        out_specs=tuple(in_vmem(5)),
        scratch_shapes=[
            pltpu.VMEM((2 * share, angles), BF16),
            pltpu.VMEM((2 * share, angles), F32),
            pltpu.SemaphoreType.DMA((3,)),
        ],
        compiler_params=params,
        name="load_own",
    )(ranks, factor, weights, current, x_near)
    partial, kept_partial, l_all = pl.pallas_call(
        functools.partial(side_kernel, share, angles),
        out_shape=(
            jax.ShapeDtypeStruct((2, 2, block, angles), BF16),
            jax.ShapeDtypeStruct((2, 2, block, angles), F32),
            jax.ShapeDtypeStruct((4 * block, leaf), BF16),
        ),
        in_specs=in_vmem(4),
        out_specs=tuple(in_vmem(3)),
        compiler_params=params,
        cost_estimate=pl.CostEstimate(flops=1 << 30, bytes_accessed=16 << 20, transcendentals=0),
        name="side_skeleton",
    )(l_own, l_x, x_own, x_core)
    partial_x = to_x(partial)
    near = pl.pallas_call(
        near_kernel,
        out_shape=jax.ShapeDtypeStruct((2, 2 * block, 2 * block), F32),
        in_specs=in_vmem(3),
        out_specs=in_vmem(1)[0],
        scratch_shapes=[pltpu.VMEM((4 * block, leaf), BF16)],
        compiler_params=params,
        cost_estimate=pl.CostEstimate(flops=20 << 30, bytes_accessed=16 << 20, transcendentals=0),
        name="near_columns",
    )(l_all, k_own, k_core)
    k_diag = to_core(k_x)
    packed = pl.pallas_call(
        between_kernel,
        out_shape=jax.ShapeDtypeStruct((2, 4, block, angles), BF16),
        in_specs=in_vmem(7),
        out_specs=in_vmem(1)[0],
        scratch_shapes=[pltpu.VMEM((4 * block, leaf), BF16)],
        compiler_params=params,
        name="between_skeletons",
    )(kept_partial, partial_x, near, keep, l_all, k_x, k_diag)
    pieces = []
    for j in range(clusters):
        held = lax.ppermute(packed, "clus", [(i, i ^ j) for i in range(clusters)]) if j else packed
        pieces += [held, to_core(held)]
    field = pl.pallas_call(
        functools.partial(chain_kernel, clusters, quarter, share, angles),
        out_shape=jax.ShapeDtypeStruct((2 * share, angles), BF16),
        in_specs=in_vmem(2 * clusters + 4),
        out_specs=in_vmem(1)[0],
        scratch_shapes=[
            pltpu.VMEM((clusters, 2 * full, full), BF16),
            pltpu.VMEM((clusters, 2, full, angles), F32),
            pltpu.VMEM((clusters, full, 2 * angles), BF16),
            pltpu.VMEM((2 * share, angles), F32),
            pltpu.VMEM((2, full, share), BF16),
        ],
        compiler_params=params,
        name="skeleton_chain",
    )(*pieces, k_own, k_x, k_core, k_diag)
    return field.reshape(share, 2, angles)


def body(excitation, leaf_factor, coupling, ranks):
    clusters, quarter, leaf = leaf_factor.shape[2:]
    share, _, angles = excitation.shape
    rows = lax.axis_size("rows")
    full = rows * clusters * quarter
    gathered = 4 * clusters * full * (angles + full)
    fits = (
        rows == 4
        and clusters == lax.axis_size("clus")
        and clusters & (clusters - 1) == 0
        and quarter == 8
        and angles == full == 128
        and share * rows == leaf
        and gathered <= SMALL_GATHER
    )
    plan = gather_body if fits else step_body
    return plan(excitation, leaf_factor, coupling, ranks)


def solution(mesh):
    placed = (
        P(("freq", "clus", "rows"), None, None),
        P("freq", "clus", None, "rows", None),
        P("freq", "clus", None, "rows", None),
        P("freq", None),
    )
    return jax.shard_map(
        body,
        mesh=mesh,
        in_specs=placed,
        out_specs=P(("freq", "clus", "rows"), None, None),
        check_vma=False,
    )
```

```python
import functools

import jax
import jax.numpy as jnp
from jax import lax
from jax.experimental import pallas as pl
from jax.experimental.pallas import tpu as pltpu
from jax.sharding import PartitionSpec as P

STEPS = 3
F32 = jnp.float32
BF16 = jnp.bfloat16
SMALL_GATHER = 4 << 20


def complex_dot(a_real, a_imag, b_real, b_imag):
    real_part = jnp.dot(a_real, b_real, preferred_element_type=F32) - jnp.dot(
        a_imag, b_imag, preferred_element_type=F32
    )
    imag_part = jnp.dot(a_real, b_imag, preferred_element_type=F32) + jnp.dot(
        a_imag, b_real, preferred_element_type=F32
    )
    return (real_part, imag_part)


def transposed_dot(columns, skel_flat):
    real_part = jnp.einsum(
        "km,kr->mr", columns[0], skel_flat[0], preferred_element_type=F32
    ) - jnp.einsum("km,kr->mr", columns[1], skel_flat[1], preferred_element_type=F32)
    imag_part = jnp.einsum(
        "km,kr->mr", columns[0], skel_flat[1], preferred_element_type=F32
    ) + jnp.einsum("km,kr->mr", columns[1], skel_flat[0], preferred_element_type=F32)
    return jnp.stack([real_part, imag_part], axis=1)


def apply_once(current, factor, weights, keep_mask, clusters, quarter, leaf_size, angles, part_row):
    gathered = lax.all_gather(current, "rows", axis=0, tiled=True)
    real_part, imag_part = complex_dot(factor[0], factor[1], gathered[:, 0], gathered[:, 1])
    skeleton = jnp.stack([real_part, imag_part]).astype(BF16).reshape(2, clusters, quarter, angles)
    received = lax.all_to_all(skeleton, "clus", split_axis=1, concat_axis=1, tiled=True)
    received = received * keep_mask[None, :, :, None]
    skel_flat = received.reshape(2, clusters * quarter, angles)
    share_rows = leaf_size // lax.axis_size("rows")
    partial_sum = transposed_dot(weights, skel_flat)
    summed = lax.psum(partial_sum, "rows")
    own_rows = lax.dynamic_slice_in_dim(summed, part_row * share_rows, share_rows, 0)
    return own_rows.astype(BF16)


def step_body(excitation, leaf_factor, coupling, ranks):
    cluster = lax.axis_index("clus")
    part_row = lax.axis_index("rows")
    clusters = leaf_factor.shape[2]
    quarter = leaf_factor.shape[3]
    leaf_size = leaf_factor.shape[4]
    angles = excitation.shape[2]
    factor = leaf_factor.reshape(2, clusters * quarter, leaf_size)
    weights = coupling.reshape(2, clusters * quarter, leaf_size)
    rank_row = lax.dynamic_slice_in_dim(ranks, cluster, 1, 0)[0]
    rank_level = part_row * quarter + jnp.arange(quarter, dtype=jnp.int32)
    keep_mask = (rank_level[None, :] < rank_row[:, None]).astype(BF16)
    current = excitation
    for step in range(STEPS):
        current = apply_once(
            current, factor, weights, keep_mask, clusters, quarter, leaf_size, angles, part_row
        )
    return current


def combine(product, rows, columns):
    real_part = product[:rows, :columns] - product[rows:, columns:]
    imag_part = product[:rows, columns:] + product[rows:, :columns]
    return real_part, imag_part


def load_kernel(
    share, angles, quarter, ranks, l_hbm, k_hbm, x_hbm, x_near,
    l_own, k_own, x_own, x_core, keep, x_flat, x_wide, sems,
):
    copies = [
        pltpu.make_async_copy(source, target, sems.at[i])
        for i, (source, target) in enumerate(((x_hbm, x_flat), (l_hbm, l_own), (k_hbm, k_own)))
    ]
    for copy in copies:
        copy.start()
    row = lax.axis_index("rows")
    cluster = lax.axis_index("clus")
    level = lax.broadcasted_iota(jnp.int32, (quarter, angles), 0)
    for at, flip in enumerate((0, 2, 1, 3)):
        base = (row ^ flip) * quarter
        for target in range(keep.shape[1] // quarter):
            below = level + base < ranks[target, cluster]
            keep[at, target * quarter : (target + 1) * quarter, :] = below.astype(F32)
    copies[0].wait()
    for source, target in ((x_flat, x_own), (x_near, x_core)):
        x_wide[...] = source[...].astype(F32)
        for part in range(2):
            target[:, part * angles : (part + 1) * angles] = x_wide[
                pl.ds(part, share, stride=2), :
            ].astype(BF16)
    copies[1].wait()
    copies[2].wait()


def side_kernel(share, angles, l_own, l_x, x_own, x_core, partial, kept_partial, l_all):
    row = lax.axis_index("rows")
    block = l_own.shape[1]
    for part in range(2):
        for at, ref in enumerate((l_own, l_x)):
            first = (2 * part + at) * block
            l_all[first : first + block, :] = ref[part]
    total = None
    for ref, quarter in ((x_own, row), (x_core, row ^ 1)):
        columns = l_all[:, pl.ds(pl.multiple_of(quarter * share, share), share)]
        term = jnp.dot(columns, ref[...], preferred_element_type=F32)
        total = term if total is None else total + term
    for part, value in enumerate(combine(total, 2 * block, angles)):
        for at in range(2):
            rows = value[at * block : (at + 1) * block]
            kept_partial[at, part] = rows
            partial[at, part] = rows.astype(BF16)


def operator_columns(l_all, k_refs, k_rows):
    block = k_refs[0].shape[1]
    for part in range(2):
        for at, ref in enumerate(k_refs):
            first = (2 * part + at) * block
            k_rows[first : first + block, :] = ref[part]
    product = lax.dot_general(
        l_all[...], k_rows[...], (((1,), (1,)), ((), ())), preferred_element_type=F32
    )
    return combine(product, 2 * block, 2 * block)


def near_kernel(l_all, k_own, k_core, near, k_rows):
    near[0], near[1] = operator_columns(l_all, (k_own, k_core), k_rows)


def far_kernel(near, keep, l_all, k_x, k_diag, between, k_rows):
    block = keep.shape[1]
    for part, far in enumerate(operator_columns(l_all, (k_x, k_diag), k_rows)):
        value = near[part]
        columns = [value[:, :block], far[:, :block], value[:, block:], far[:, block:]]
        value = jnp.concatenate(columns, axis=1)
        for at in range(2):
            between[at, part] = (value[at * block : (at + 1) * block] * keep[at]).astype(BF16)


def pack_kernel(partial, partial_x, keep, between, packed):
    for at in range(2):
        for part in range(2):
            value = partial[at, part] + partial_x[1 - at, part].astype(F32)
            packed[at, part] = (value * keep[at]).astype(BF16)
            packed[at, 2 + part] = between[at, part]


def fold_kernel(share, k_own, k_x, k_core, k_diag, folded, wide):
    row = lax.axis_index("rows")
    mine = pl.ds(pl.multiple_of(row * share, share), share)
    real, imag = (
        jnp.concatenate([k[part, :, mine].astype(F32) for k in (k_own, k_x, k_core, k_diag)], axis=0).T
        for part in range(2)
    )
    full = real.shape[1]
    even, odd = pl.ds(0, share, stride=2), pl.ds(1, share, stride=2)
    wide[0, even, :] = real
    wide[1, even, :] = -imag
    wide[0, odd, :] = imag
    wide[1, odd, :] = real
    folded[:, :full] = wide[0].astype(BF16)
    folded[:, full:] = wide[1].astype(BF16)


def chain_kernel(clusters, quarter, *refs):
    pieces, folded, field = refs[: 2 * clusters], refs[2 * clusters], refs[2 * clusters + 1]
    between, skeleton, kept = refs[2 * clusters + 2 :]
    cluster = lax.axis_index("clus")
    block = clusters * quarter
    full = 4 * block
    for j in range(clusters):
        source = cluster ^ j
        for core in range(2):
            ref = pieces[2 * j + core]
            for at in range(2):
                first = (2 * core + at) * block
                rows = slice(first, first + block)
                for part in range(2):
                    columns = slice(part * full, (part + 1) * full)
                    skeleton[source, rows, columns] = ref[at, part].astype(F32)
                    value = ref[at, 2 + part]
                    if core:
                        value = pltpu.roll(value.astype(F32), full // 2, 1).astype(BF16)
                    between[source, rows, columns] = value

    def gather(target):
        rows = [
            skeleton[s, pl.ds(pl.multiple_of(q * block + target * quarter, quarter), quarter), :]
            for q in range(4)
            for s in range(clusters)
        ]
        return jnp.concatenate(rows, axis=0)

    for step in range(STEPS - 1):
        for target in range(clusters):
            value = gather(target)
            kept[target, :full, :] = value.astype(BF16)
            kept[target, full:, :full] = (-value[:, full:]).astype(BF16)
            kept[target, full:, full:] = value[:, :full].astype(BF16)
        for source in range(clusters):
            skeleton[source] = jnp.dot(between[source], kept[source], preferred_element_type=F32)
    value = gather(cluster)
    last = jnp.concatenate([value[:, :full], value[:, full:]], axis=0).astype(BF16)
    field[...] = jnp.dot(folded[...], last, preferred_element_type=F32).astype(BF16)


def in_vmem(count):
    return [pl.BlockSpec(memory_space=pltpu.VMEM)] * count


def gather_body(excitation, leaf_factor, coupling, ranks):
    clusters, quarter, leaf = leaf_factor.shape[2:]
    share, _, angles = excitation.shape
    block = clusters * quarter
    full = 4 * block
    params = pltpu.CompilerParams(vmem_limit_bytes=32 << 20)

    def across(flip):
        return lambda v: lax.ppermute(v, "rows", [(i, i ^ flip) for i in range(4)])

    to_x, to_core = across(2), across(1)
    factor = leaf_factor.reshape(2, block, leaf)
    weights = coupling.reshape(2, block, leaf)
    l_x, k_x = to_x(factor), to_x(weights)
    current = excitation.reshape(2 * share, angles)
    x_near = to_core(current)
    k_core = to_core(weights)
    l_own, k_own, x_own, x_core, keep = pl.pallas_call(
        functools.partial(load_kernel, share, angles, quarter),
        out_shape=(
            jax.ShapeDtypeStruct(factor.shape, BF16),
            jax.ShapeDtypeStruct(weights.shape, BF16),
            jax.ShapeDtypeStruct((share, 2 * angles), BF16),
            jax.ShapeDtypeStruct((share, 2 * angles), BF16),
            jax.ShapeDtypeStruct((4, block, angles), F32),
        ),
        in_specs=[pl.BlockSpec(memory_space=pltpu.SMEM)]
        + [pl.BlockSpec(memory_space=pl.ANY)] * 3
        + in_vmem(1),
        out_specs=tuple(in_vmem(5)),
        scratch_shapes=[
            pltpu.VMEM((2 * share, angles), BF16),
            pltpu.VMEM((2 * share, angles), F32),
            pltpu.SemaphoreType.DMA((3,)),
        ],
        compiler_params=params,
        name="load_own",
    )(ranks, factor, weights, current, x_near)
    partial, kept_partial, l_all = pl.pallas_call(
        functools.partial(side_kernel, share, angles),
        out_shape=(
            jax.ShapeDtypeStruct((2, 2, block, angles), BF16),
            jax.ShapeDtypeStruct((2, 2, block, angles), F32),
            jax.ShapeDtypeStruct((4 * block, leaf), BF16),
        ),
        in_specs=in_vmem(4),
        out_specs=tuple(in_vmem(3)),
        compiler_params=params,
        cost_estimate=pl.CostEstimate(flops=1 << 30, bytes_accessed=16 << 20, transcendentals=0),
        name="side_skeleton",
    )(l_own, l_x, x_own, x_core)
    partial_x = to_x(partial)
    near = pl.pallas_call(
        near_kernel,
        out_shape=jax.ShapeDtypeStruct((2, 2 * block, 2 * block), F32),
        in_specs=in_vmem(3),
        out_specs=in_vmem(1)[0],
        scratch_shapes=[pltpu.VMEM((4 * block, leaf), BF16)],
        compiler_params=params,
        cost_estimate=pl.CostEstimate(flops=20 << 30, bytes_accessed=16 << 20, transcendentals=0),
        name="near_columns",
    )(l_all, k_own, k_core)
    k_diag = to_core(k_x)
    between = pl.pallas_call(
        far_kernel,
        out_shape=jax.ShapeDtypeStruct((2, 2, block, full), BF16),
        in_specs=in_vmem(5),
        out_specs=in_vmem(1)[0],
        scratch_shapes=[pltpu.VMEM((4 * block, leaf), BF16)],
        compiler_params=params,
        name="far_columns",
    )(near, keep, l_all, k_x, k_diag)
    packed = pl.pallas_call(
        pack_kernel,
        out_shape=jax.ShapeDtypeStruct((2, 4, block, angles), BF16),
        in_specs=in_vmem(4),
        out_specs=in_vmem(1)[0],
        compiler_params=params,
        name="pack_rows",
    )(kept_partial, partial_x, keep, between)
    folded = pl.pallas_call(
        functools.partial(fold_kernel, share),
        out_shape=jax.ShapeDtypeStruct((2 * share, 2 * full), BF16),
        in_specs=in_vmem(4),
        out_specs=in_vmem(1)[0],
        scratch_shapes=[pltpu.VMEM((2, 2 * share, full), F32)],
        compiler_params=params,
        name="fold_coupling",
    )(k_own, k_x, k_core, k_diag)
    held = {0: packed}
    for j in range(1, clusters):
        held[j] = lax.ppermute(packed, "clus", [(i, i ^ j) for i in range(clusters)])
    pieces = []
    for j in range(clusters):
        pieces += [held[j], to_core(held[j])]
    field = pl.pallas_call(
        functools.partial(chain_kernel, clusters, quarter),
        out_shape=jax.ShapeDtypeStruct((2 * share, angles), BF16),
        in_specs=in_vmem(2 * clusters + 1),
        out_specs=in_vmem(1)[0],
        scratch_shapes=[
            pltpu.VMEM((clusters, full, 2 * full), BF16),
            pltpu.VMEM((clusters, full, 2 * angles), F32),
            pltpu.VMEM((clusters, 2 * full, 2 * angles), BF16),
        ],
        compiler_params=params,
        name="skeleton_chain",
    )(*pieces, folded)
    return field.reshape(share, 2, angles)


def body(excitation, leaf_factor, coupling, ranks):
    clusters, quarter, leaf = leaf_factor.shape[2:]
    share, _, angles = excitation.shape
    rows = lax.axis_size("rows")
    full = rows * clusters * quarter
    gathered = 4 * clusters * full * (angles + full)
    fits = (
        rows == 4
        and clusters == lax.axis_size("clus")
        and clusters & (clusters - 1) == 0
        and quarter == 8
        and angles == full == 128
        and share * rows == leaf
        and gathered <= SMALL_GATHER
    )
    plan = gather_body if fits else step_body
    return plan(excitation, leaf_factor, coupling, ranks)


def solution(mesh):
    placed = (
        P(("freq", "clus", "rows"), None, None),
        P("freq", "clus", None, "rows", None),
        P("freq", "clus", None, "rows", None),
        P("freq", None),
    )
    return jax.shard_map(
        body,
        mesh=mesh,
        in_specs=placed,
        out_specs=P(("freq", "clus", "rows"), None, None),
        check_vma=False,
    )
```

```python
import functools

import jax
import jax.numpy as jnp
from jax import lax
from jax.experimental import pallas as pl
from jax.experimental.pallas import tpu as pltpu
from jax.sharding import PartitionSpec as P

STEPS = 3
F32 = jnp.float32
BF16 = jnp.bfloat16
SMALL_GATHER = 4 << 20
ROUNDS = ((0, 1, 2, 3), (2, 0, 3, 1), (1, 3, 0, 2), (3, 2, 1, 0))


def complex_dot(a_real, a_imag, b_real, b_imag):
    real_part = jnp.dot(a_real, b_real, preferred_element_type=F32) - jnp.dot(
        a_imag, b_imag, preferred_element_type=F32
    )
    imag_part = jnp.dot(a_real, b_imag, preferred_element_type=F32) + jnp.dot(
        a_imag, b_real, preferred_element_type=F32
    )
    return (real_part, imag_part)


def transposed_dot(columns, skel_flat):
    real_part = jnp.einsum(
        "km,kr->mr", columns[0], skel_flat[0], preferred_element_type=F32
    ) - jnp.einsum("km,kr->mr", columns[1], skel_flat[1], preferred_element_type=F32)
    imag_part = jnp.einsum(
        "km,kr->mr", columns[0], skel_flat[1], preferred_element_type=F32
    ) + jnp.einsum("km,kr->mr", columns[1], skel_flat[0], preferred_element_type=F32)
    return jnp.stack([real_part, imag_part], axis=1)


def apply_once(current, factor, weights, keep_mask, clusters, quarter, leaf_size, angles, part_row):
    gathered = lax.all_gather(current, "rows", axis=0, tiled=True)
    real_part, imag_part = complex_dot(factor[0], factor[1], gathered[:, 0], gathered[:, 1])
    skeleton = jnp.stack([real_part, imag_part]).astype(BF16).reshape(2, clusters, quarter, angles)
    received = lax.all_to_all(skeleton, "clus", split_axis=1, concat_axis=1, tiled=True)
    received = received * keep_mask[None, :, :, None]
    skel_flat = received.reshape(2, clusters * quarter, angles)
    share_rows = leaf_size // lax.axis_size("rows")
    partial_sum = transposed_dot(weights, skel_flat)
    summed = lax.psum(partial_sum, "rows")
    own_rows = lax.dynamic_slice_in_dim(summed, part_row * share_rows, share_rows, 0)
    return own_rows.astype(BF16)


def step_body(excitation, leaf_factor, coupling, ranks):
    cluster = lax.axis_index("clus")
    part_row = lax.axis_index("rows")
    clusters = leaf_factor.shape[2]
    quarter = leaf_factor.shape[3]
    leaf_size = leaf_factor.shape[4]
    angles = excitation.shape[2]
    factor = leaf_factor.reshape(2, clusters * quarter, leaf_size)
    weights = coupling.reshape(2, clusters * quarter, leaf_size)
    rank_row = lax.dynamic_slice_in_dim(ranks, cluster, 1, 0)[0]
    rank_level = part_row * quarter + jnp.arange(quarter, dtype=jnp.int32)
    keep_mask = (rank_level[None, :] < rank_row[:, None]).astype(BF16)
    current = excitation
    for step in range(STEPS):
        current = apply_once(
            current, factor, weights, keep_mask, clusters, quarter, leaf_size, angles, part_row
        )
    return current


def combine(product, rows, columns):
    real_part = product[:rows, :columns] - product[rows:, columns:]
    imag_part = product[:rows, columns:] + product[rows:, :columns]
    return real_part, imag_part


def load_kernel(
    share, angles, quarter, ranks, l_hbm, k_hbm, x_hbm, x_near,
    l_own, k_own, x_own, x_core, keep, x_flat, x_wide, sems,
):
    copies = [
        pltpu.make_async_copy(source, target, sems.at[i])
        for i, (source, target) in enumerate(((x_hbm, x_flat), (l_hbm, l_own), (k_hbm, k_own)))
    ]
    for copy in copies:
        copy.start()
    row = lax.axis_index("rows")
    cluster = lax.axis_index("clus")
    level = lax.broadcasted_iota(jnp.int32, (quarter, angles), 0)
    for at, flip in enumerate((0, 2, 1, 3)):
        base = (row ^ flip) * quarter
        for target in range(keep.shape[1] // quarter):
            below = level + base < ranks[target, cluster]
            keep[at, target * quarter : (target + 1) * quarter, :] = below.astype(F32)
    copies[0].wait()
    for source, target in ((x_flat, x_own), (x_near, x_core)):
        x_wide[...] = source[...].astype(F32)
        for part in range(2):
            target[:, part * angles : (part + 1) * angles] = x_wide[
                pl.ds(part, share, stride=2), :
            ].astype(BF16)
    copies[1].wait()
    copies[2].wait()


def side_kernel(share, angles, l_own, l_x, x_own, x_core, partial, kept_partial, l_all):
    row = lax.axis_index("rows")
    block = l_own.shape[1]
    for part in range(2):
        for at, ref in enumerate((l_own, l_x)):
            first = (2 * part + at) * block
            l_all[first : first + block, :] = ref[part]
    total = None
    for ref, quarter in ((x_own, row), (x_core, row ^ 1)):
        columns = l_all[:, pl.ds(pl.multiple_of(quarter * share, share), share)]
        term = jnp.dot(columns, ref[...], preferred_element_type=F32)
        total = term if total is None else total + term
    for part, value in enumerate(combine(total, 2 * block, angles)):
        for at in range(2):
            rows = value[at * block : (at + 1) * block]
            kept_partial[at, part] = rows
            partial[at, part] = rows.astype(BF16)


def operator_columns(l_all, k_refs, k_rows):
    block = k_refs[0].shape[1]
    for part in range(2):
        for at, ref in enumerate(k_refs):
            first = (2 * part + at) * block
            k_rows[first : first + block, :] = ref[part]
    product = lax.dot_general(
        l_all[...], k_rows[...], (((1,), (1,)), ((), ())), preferred_element_type=F32
    )
    return combine(product, 2 * block, 2 * block)


def near_kernel(l_all, k_own, k_core, near, k_rows):
    near[0], near[1] = operator_columns(l_all, (k_own, k_core), k_rows)


def far_kernel(near, keep, l_all, k_x, k_diag, between, k_rows):
    block = keep.shape[1]
    for part, far in enumerate(operator_columns(l_all, (k_x, k_diag), k_rows)):
        value = near[part]
        columns = [value[:, :block], far[:, :block], value[:, block:], far[:, block:]]
        value = jnp.concatenate(columns, axis=1)
        for at in range(2):
            between[at, part] = (value[at * block : (at + 1) * block] * keep[at]).astype(BF16)


def pack_kernel(partial, partial_x, keep, between, packed):
    for at in range(2):
        for part in range(2):
            value = partial[at, part] + partial_x[1 - at, part].astype(F32)
            packed[at, part] = (value * keep[at]).astype(BF16)
            packed[at, 2 + part] = between[at, part]


def fold_kernel(share, k_own, k_x, k_core, k_diag, folded, wide):
    row = lax.axis_index("rows")
    mine = pl.ds(pl.multiple_of(row * share, share), share)
    real, imag = (
        jnp.concatenate([k[part, :, mine].astype(F32) for k in (k_own, k_x, k_core, k_diag)], axis=0).T
        for part in range(2)
    )
    full = real.shape[1]
    even, odd = pl.ds(0, share, stride=2), pl.ds(1, share, stride=2)
    wide[0, even, :] = real
    wide[1, even, :] = -imag
    wide[0, odd, :] = imag
    wide[1, odd, :] = real
    folded[:, :full] = wide[0].astype(BF16)
    folded[:, full:] = wide[1].astype(BF16)


def sender(targets, cluster):
    source = jnp.int32(0)
    for at, target in enumerate(targets):
        source = jnp.where(cluster == target, at, source)
    return source


def chain_kernel(clusters, quarter, *refs):
    pieces, folded, field = refs[: 2 * clusters], refs[2 * clusters], refs[2 * clusters + 1]
    between, skeleton, kept = refs[2 * clusters + 2 :]
    cluster = lax.axis_index("clus")
    block = clusters * quarter
    full = 4 * block
    for j in range(clusters):
        source = sender(ROUNDS[j], cluster)
        for core in range(2):
            ref = pieces[2 * j + core]
            for at in range(2):
                first = (2 * core + at) * block
                rows = slice(first, first + block)
                for part in range(2):
                    columns = slice(part * full, (part + 1) * full)
                    skeleton[source, rows, columns] = ref[at, part].astype(F32)
                    value = ref[at, 2 + part]
                    if core:
                        value = pltpu.roll(value.astype(F32), full // 2, 1).astype(BF16)
                    between[source, rows, columns] = value

    def gather(target):
        rows = [
            skeleton[s, pl.ds(pl.multiple_of(q * block + target * quarter, quarter), quarter), :]
            for q in range(4)
            for s in range(clusters)
        ]
        return jnp.concatenate(rows, axis=0)

    def embed(target, value):
        kept[target, :full, :] = value.astype(BF16)
        kept[target, full:, :full] = (-value[:, full:]).astype(BF16)
        kept[target, full:, full:] = value[:, :full].astype(BF16)

    def own_target(source):
        blocks = []
        for q in range(4):
            rows = between[source, q * block : (q + 1) * block, :].astype(F32)
            chosen = rows[:quarter]
            for target in range(1, clusters):
                other = rows[target * quarter : (target + 1) * quarter]
                chosen = jnp.where(cluster == target, other, chosen)
            blocks.append(chosen)
        return jnp.concatenate(blocks, axis=0).astype(BF16)

    for target in range(clusters):
        embed(target, gather(target))
    for step in range(STEPS - 2):
        for source in range(clusters):
            skeleton[source] = jnp.dot(between[source], kept[source], preferred_element_type=F32)
        for target in range(clusters):
            embed(target, gather(target))
    wanted = [
        jnp.dot(own_target(source), kept[source], preferred_element_type=F32)
        for source in range(clusters)
    ]
    value = jnp.concatenate(
        [wanted[s][q * quarter : (q + 1) * quarter] for q in range(4) for s in range(clusters)], axis=0
    )
    last = jnp.concatenate([value[:, :full], value[:, full:]], axis=0).astype(BF16)
    field[...] = jnp.dot(folded[...], last, preferred_element_type=F32).astype(BF16)


def in_vmem(count):
    return [pl.BlockSpec(memory_space=pltpu.VMEM)] * count


def gather_body(excitation, leaf_factor, coupling, ranks):
    clusters, quarter, leaf = leaf_factor.shape[2:]
    share, _, angles = excitation.shape
    block = clusters * quarter
    full = 4 * block
    params = pltpu.CompilerParams(vmem_limit_bytes=32 << 20)

    def across(flip):
        return lambda v: lax.ppermute(v, "rows", [(i, i ^ flip) for i in range(4)])

    to_x, to_core = across(2), across(1)
    factor = leaf_factor.reshape(2, block, leaf)
    weights = coupling.reshape(2, block, leaf)
    l_x, k_x = to_x(factor), to_x(weights)
    current = excitation.reshape(2 * share, angles)
    x_near = to_core(current)
    k_core = to_core(weights)
    l_own, k_own, x_own, x_core, keep = pl.pallas_call(
        functools.partial(load_kernel, share, angles, quarter),
        out_shape=(
            jax.ShapeDtypeStruct(factor.shape, BF16),
            jax.ShapeDtypeStruct(weights.shape, BF16),
            jax.ShapeDtypeStruct((share, 2 * angles), BF16),
            jax.ShapeDtypeStruct((share, 2 * angles), BF16),
            jax.ShapeDtypeStruct((4, block, angles), F32),
        ),
        in_specs=[pl.BlockSpec(memory_space=pltpu.SMEM)]
        + [pl.BlockSpec(memory_space=pl.ANY)] * 3
        + in_vmem(1),
        out_specs=tuple(in_vmem(5)),
        scratch_shapes=[
            pltpu.VMEM((2 * share, angles), BF16),
            pltpu.VMEM((2 * share, angles), F32),
            pltpu.SemaphoreType.DMA((3,)),
        ],
        compiler_params=params,
        name="load_own",
    )(ranks, factor, weights, current, x_near)
    partial, kept_partial, l_all = pl.pallas_call(
        functools.partial(side_kernel, share, angles),
        out_shape=(
            jax.ShapeDtypeStruct((2, 2, block, angles), BF16),
            jax.ShapeDtypeStruct((2, 2, block, angles), F32),
            jax.ShapeDtypeStruct((4 * block, leaf), BF16),
        ),
        in_specs=in_vmem(4),
        out_specs=tuple(in_vmem(3)),
        compiler_params=params,
        cost_estimate=pl.CostEstimate(flops=1 << 30, bytes_accessed=16 << 20, transcendentals=0),
        name="side_skeleton",
    )(l_own, l_x, x_own, x_core)
    partial_x = to_x(partial)
    near = pl.pallas_call(
        near_kernel,
        out_shape=jax.ShapeDtypeStruct((2, 2 * block, 2 * block), F32),
        in_specs=in_vmem(3),
        out_specs=in_vmem(1)[0],
        scratch_shapes=[pltpu.VMEM((4 * block, leaf), BF16)],
        compiler_params=params,
        cost_estimate=pl.CostEstimate(flops=20 << 30, bytes_accessed=16 << 20, transcendentals=0),
        name="near_columns",
    )(l_all, k_own, k_core)
    k_diag = to_core(k_x)
    between = pl.pallas_call(
        far_kernel,
        out_shape=jax.ShapeDtypeStruct((2, 2, block, full), BF16),
        in_specs=in_vmem(5),
        out_specs=in_vmem(1)[0],
        scratch_shapes=[pltpu.VMEM((4 * block, leaf), BF16)],
        compiler_params=params,
        name="far_columns",
    )(near, keep, l_all, k_x, k_diag)
    packed = pl.pallas_call(
        pack_kernel,
        out_shape=jax.ShapeDtypeStruct((2, 4, block, angles), BF16),
        in_specs=in_vmem(4),
        out_specs=in_vmem(1)[0],
        compiler_params=params,
        name="pack_rows",
    )(kept_partial, partial_x, keep, between)
    folded = pl.pallas_call(
        functools.partial(fold_kernel, share),
        out_shape=jax.ShapeDtypeStruct((2 * share, 2 * full), BF16),
        in_specs=in_vmem(4),
        out_specs=in_vmem(1)[0],
        scratch_shapes=[pltpu.VMEM((2, 2 * share, full), F32)],
        compiler_params=params,
        name="fold_coupling",
    )(k_own, k_x, k_core, k_diag)
    held = {0: packed}
    for j in range(1, clusters):
        held[j] = lax.ppermute(packed, "clus", list(enumerate(ROUNDS[j])))
    pieces = []
    for j in range(clusters):
        pieces += [held[j], to_core(held[j])]
    field = pl.pallas_call(
        functools.partial(chain_kernel, clusters, quarter),
        out_shape=jax.ShapeDtypeStruct((2 * share, angles), BF16),
        in_specs=in_vmem(2 * clusters + 1),
        out_specs=in_vmem(1)[0],
        scratch_shapes=[
            pltpu.VMEM((clusters, full, 2 * full), BF16),
            pltpu.VMEM((clusters, full, 2 * angles), F32),
            pltpu.VMEM((clusters, 2 * full, 2 * angles), BF16),
        ],
        compiler_params=params,
        name="skeleton_chain",
    )(*pieces, folded)
    return field.reshape(share, 2, angles)


def body(excitation, leaf_factor, coupling, ranks):
    clusters, quarter, leaf = leaf_factor.shape[2:]
    share, _, angles = excitation.shape
    rows = lax.axis_size("rows")
    full = rows * clusters * quarter
    gathered = 4 * clusters * full * (angles + full)
    fits = (
        rows == 4
        and clusters == lax.axis_size("clus")
        and clusters == len(ROUNDS)
        and quarter == 8
        and angles == full == 128
        and share * rows == leaf
        and gathered <= SMALL_GATHER
    )
    plan = gather_body if fits else step_body
    return plan(excitation, leaf_factor, coupling, ranks)


def solution(mesh):
    placed = (
        P(("freq", "clus", "rows"), None, None),
        P("freq", "clus", None, "rows", None),
        P("freq", "clus", None, "rows", None),
        P("freq", None),
    )
    return jax.shard_map(
        body,
        mesh=mesh,
        in_specs=placed,
        out_specs=P(("freq", "clus", "rows"), None, None),
        check_vma=False,
    )
```

```python
import functools

import jax
import jax.numpy as jnp
from jax import lax
from jax.experimental import pallas as pl
from jax.experimental.pallas import tpu as pltpu
from jax.sharding import PartitionSpec as P

STEPS = 3
F32 = jnp.float32
BF16 = jnp.bfloat16
SMALL_GATHER = 4 << 20
ROUNDS = (
    ((0, 1, 2, 3), (2, 0, 3, 1), (1, 3, 0, 2), (3, 2, 1, 0)),
    ((0, 1, 2, 3), (3, 0, 1, 2), (1, 2, 3, 0), (2, 3, 0, 1)),
)


def complex_dot(a_real, a_imag, b_real, b_imag):
    real_part = jnp.dot(a_real, b_real, preferred_element_type=F32) - jnp.dot(
        a_imag, b_imag, preferred_element_type=F32
    )
    imag_part = jnp.dot(a_real, b_imag, preferred_element_type=F32) + jnp.dot(
        a_imag, b_real, preferred_element_type=F32
    )
    return (real_part, imag_part)


def transposed_dot(columns, skel_flat):
    real_part = jnp.einsum(
        "km,kr->mr", columns[0], skel_flat[0], preferred_element_type=F32
    ) - jnp.einsum("km,kr->mr", columns[1], skel_flat[1], preferred_element_type=F32)
    imag_part = jnp.einsum(
        "km,kr->mr", columns[0], skel_flat[1], preferred_element_type=F32
    ) + jnp.einsum("km,kr->mr", columns[1], skel_flat[0], preferred_element_type=F32)
    return jnp.stack([real_part, imag_part], axis=1)


def apply_once(current, factor, weights, keep_mask, clusters, quarter, leaf_size, angles, part_row):
    gathered = lax.all_gather(current, "rows", axis=0, tiled=True)
    real_part, imag_part = complex_dot(factor[0], factor[1], gathered[:, 0], gathered[:, 1])
    skeleton = jnp.stack([real_part, imag_part]).astype(BF16).reshape(2, clusters, quarter, angles)
    received = lax.all_to_all(skeleton, "clus", split_axis=1, concat_axis=1, tiled=True)
    received = received * keep_mask[None, :, :, None]
    skel_flat = received.reshape(2, clusters * quarter, angles)
    share_rows = leaf_size // lax.axis_size("rows")
    partial_sum = transposed_dot(weights, skel_flat)
    summed = lax.psum(partial_sum, "rows")
    own_rows = lax.dynamic_slice_in_dim(summed, part_row * share_rows, share_rows, 0)
    return own_rows.astype(BF16)


def step_body(excitation, leaf_factor, coupling, ranks):
    cluster = lax.axis_index("clus")
    part_row = lax.axis_index("rows")
    clusters = leaf_factor.shape[2]
    quarter = leaf_factor.shape[3]
    leaf_size = leaf_factor.shape[4]
    angles = excitation.shape[2]
    factor = leaf_factor.reshape(2, clusters * quarter, leaf_size)
    weights = coupling.reshape(2, clusters * quarter, leaf_size)
    rank_row = lax.dynamic_slice_in_dim(ranks, cluster, 1, 0)[0]
    rank_level = part_row * quarter + jnp.arange(quarter, dtype=jnp.int32)
    keep_mask = (rank_level[None, :] < rank_row[:, None]).astype(BF16)
    current = excitation
    for step in range(STEPS):
        current = apply_once(
            current, factor, weights, keep_mask, clusters, quarter, leaf_size, angles, part_row
        )
    return current


def combine(product, rows, columns):
    real_part = product[:rows, :columns] - product[rows:, columns:]
    imag_part = product[:rows, columns:] + product[rows:, :columns]
    return real_part, imag_part


def load_kernel(
    share, angles, quarter, ranks, l_hbm, x_hbm, x_near,
    l_own, x_own, x_core, keep, x_flat, x_wide, sems,
):
    copies = [
        pltpu.make_async_copy(source, target, sems.at[i])
        for i, (source, target) in enumerate(((x_hbm, x_flat), (l_hbm, l_own)))
    ]
    for copy in copies:
        copy.start()
    row = lax.axis_index("rows")
    cluster = lax.axis_index("clus")
    level = lax.broadcasted_iota(jnp.int32, (quarter, angles), 0)
    for at, flip in enumerate((0, 2, 1, 3)):
        base = (row ^ flip) * quarter
        for target in range(keep.shape[1] // quarter):
            below = level + base < ranks[target, cluster]
            keep[at, target * quarter : (target + 1) * quarter, :] = below.astype(F32)
    copies[0].wait()
    for source, target in ((x_flat, x_own), (x_near, x_core)):
        x_wide[...] = source[...].astype(F32)
        for part in range(2):
            target[:, part * angles : (part + 1) * angles] = x_wide[
                pl.ds(part, share, stride=2), :
            ].astype(BF16)
    copies[1].wait()


def side_kernel(share, angles, l_own, l_x, x_own, x_core, partial, kept_partial, l_all):
    row = lax.axis_index("rows")
    block = l_own.shape[1]
    for part in range(2):
        for at, ref in enumerate((l_own, l_x)):
            first = (2 * part + at) * block
            l_all[first : first + block, :] = ref[part]
    total = None
    for ref, quarter in ((x_own, row), (x_core, row ^ 1)):
        columns = l_all[:, pl.ds(pl.multiple_of(quarter * share, share), share)]
        term = jnp.dot(columns, ref[...], preferred_element_type=F32)
        total = term if total is None else total + term
    for part, value in enumerate(combine(total, 2 * block, angles)):
        for at in range(2):
            rows = value[at * block : (at + 1) * block]
            kept_partial[at, part] = rows
            partial[at, part] = rows.astype(BF16)


def operator_columns(l_all, k_refs, k_rows):
    block = k_refs[0].shape[1]
    for part in range(2):
        for at, ref in enumerate(k_refs):
            first = (2 * part + at) * block
            k_rows[first : first + block, :] = ref[part]
    product = lax.dot_general(
        l_all[...], k_rows[...], (((1,), (1,)), ((), ())), preferred_element_type=F32
    )
    return combine(product, 2 * block, 2 * block)


def near_kernel(l_all, k_own, k_core, near, k_rows):
    near[0], near[1] = operator_columns(l_all, (k_own, k_core), k_rows)


def far_kernel(near, keep, l_all, k_x, k_diag, between, k_rows):
    block = keep.shape[1]
    for part, far in enumerate(operator_columns(l_all, (k_x, k_diag), k_rows)):
        value = near[part]
        columns = [value[:, :block], far[:, :block], value[:, block:], far[:, block:]]
        value = jnp.concatenate(columns, axis=1)
        for at in range(2):
            between[at, part] = (value[at * block : (at + 1) * block] * keep[at]).astype(BF16)


def pack_kernel(partial, partial_x, keep, between, packed):
    for at in range(2):
        for part in range(2):
            value = partial[at, part] + partial_x[1 - at, part].astype(F32)
            packed[at, part] = (value * keep[at]).astype(BF16)
            packed[at, 2 + part] = between[at, part]


def fold_kernel(share, k_own, k_x, k_core, k_diag, folded, wide):
    row = lax.axis_index("rows")
    mine = pl.ds(pl.multiple_of(row * share, share), share)
    real, imag = (
        jnp.concatenate([k[part, :, mine].astype(F32) for k in (k_own, k_x, k_core, k_diag)], axis=0).T
        for part in range(2)
    )
    full = real.shape[1]
    even, odd = pl.ds(0, share, stride=2), pl.ds(1, share, stride=2)
    wide[0, even, :] = real
    wide[1, even, :] = -imag
    wide[0, odd, :] = imag
    wide[1, odd, :] = real
    folded[:, :full] = wide[0].astype(BF16)
    folded[:, full:] = wide[1].astype(BF16)


def sender(targets, cluster):
    source = jnp.int32(0)
    for at, target in enumerate(targets):
        source = jnp.where(cluster == target, at, source)
    return source


def chain_kernel(clusters, quarter, *refs):
    pieces, folded, field = refs[: 2 * clusters], refs[2 * clusters], refs[2 * clusters + 1]
    between, skeleton, kept = refs[2 * clusters + 2 :]
    row = lax.axis_index("rows")
    cluster = lax.axis_index("clus")
    block = clusters * quarter
    full = 4 * block
    for j in range(clusters):
        senders = [sender(rounds[j], cluster) for rounds in ROUNDS]
        for core in range(2):
            source = jnp.where(row % 2 == core, senders[0], senders[1])
            ref = pieces[2 * j + core]
            for at in range(2):
                first = (2 * core + at) * block
                rows = slice(first, first + block)
                for part in range(2):
                    columns = slice(part * full, (part + 1) * full)
                    skeleton[source, rows, columns] = ref[at, part].astype(F32)
                    value = ref[at, 2 + part]
                    if core:
                        value = pltpu.roll(value.astype(F32), full // 2, 1).astype(BF16)
                    between[source, rows, columns] = value

    def gather(target):
        rows = [
            skeleton[s, pl.ds(pl.multiple_of(q * block + target * quarter, quarter), quarter), :]
            for q in range(4)
            for s in range(clusters)
        ]
        return jnp.concatenate(rows, axis=0)

    def embed(target, value):
        kept[target, :full, :] = value.astype(BF16)
        kept[target, full:, :full] = (-value[:, full:]).astype(BF16)
        kept[target, full:, full:] = value[:, :full].astype(BF16)

    def own_target(source):
        blocks = []
        for q in range(4):
            rows = between[source, q * block : (q + 1) * block, :].astype(F32)
            chosen = rows[:quarter]
            for target in range(1, clusters):
                other = rows[target * quarter : (target + 1) * quarter]
                chosen = jnp.where(cluster == target, other, chosen)
            blocks.append(chosen)
        return jnp.concatenate(blocks, axis=0).astype(BF16)

    for target in range(clusters):
        embed(target, gather(target))
    for step in range(STEPS - 2):
        for source in range(clusters):
            skeleton[source] = jnp.dot(between[source], kept[source], preferred_element_type=F32)
        for target in range(clusters):
            embed(target, gather(target))
    wanted = [
        jnp.dot(own_target(source), kept[source], preferred_element_type=F32)
        for source in range(clusters)
    ]
    value = jnp.concatenate(
        [wanted[s][q * quarter : (q + 1) * quarter] for q in range(4) for s in range(clusters)], axis=0
    )
    last = jnp.concatenate([value[:, :full], value[:, full:]], axis=0).astype(BF16)
    field[...] = jnp.dot(folded[...], last, preferred_element_type=F32).astype(BF16)


def in_vmem(count):
    return [pl.BlockSpec(memory_space=pltpu.VMEM)] * count


def gather_body(excitation, leaf_factor, coupling, ranks):
    clusters, quarter, leaf = leaf_factor.shape[2:]
    share, _, angles = excitation.shape
    block = clusters * quarter
    full = 4 * block
    params = pltpu.CompilerParams(vmem_limit_bytes=32 << 20)

    def across(flip):
        return lambda v: lax.ppermute(v, "rows", [(i, i ^ flip) for i in range(4)])

    to_x, to_core = across(2), across(1)
    factor = leaf_factor.reshape(2, block, leaf)
    weights = coupling.reshape(2, block, leaf)
    l_x = to_x(factor)
    current = excitation.reshape(2 * share, angles)
    x_near = to_core(current)
    to_send, _ = lax.optimization_barrier((weights, x_near))
    k_x = to_x(to_send)
    k_core = to_core(weights)
    l_own, x_own, x_core, keep = pl.pallas_call(
        functools.partial(load_kernel, share, angles, quarter),
        out_shape=(
            jax.ShapeDtypeStruct(factor.shape, BF16),
            jax.ShapeDtypeStruct((share, 2 * angles), BF16),
            jax.ShapeDtypeStruct((share, 2 * angles), BF16),
            jax.ShapeDtypeStruct((4, block, angles), F32),
        ),
        in_specs=[pl.BlockSpec(memory_space=pltpu.SMEM)]
        + [pl.BlockSpec(memory_space=pl.ANY)] * 2
        + in_vmem(1),
        out_specs=tuple(in_vmem(4)),
        scratch_shapes=[
            pltpu.VMEM((2 * share, angles), BF16),
            pltpu.VMEM((2 * share, angles), F32),
            pltpu.SemaphoreType.DMA((2,)),
        ],
        compiler_params=params,
        name="load_own",
    )(ranks, factor, current, x_near)
    partial, kept_partial, l_all = pl.pallas_call(
        functools.partial(side_kernel, share, angles),
        out_shape=(
            jax.ShapeDtypeStruct((2, 2, block, angles), BF16),
            jax.ShapeDtypeStruct((2, 2, block, angles), F32),
            jax.ShapeDtypeStruct((4 * block, leaf), BF16),
        ),
        in_specs=in_vmem(4),
        out_specs=tuple(in_vmem(3)),
        compiler_params=params,
        cost_estimate=pl.CostEstimate(flops=1 << 30, bytes_accessed=16 << 20, transcendentals=0),
        name="side_skeleton",
    )(l_own, l_x, x_own, x_core)
    partial_x = to_x(partial)
    near = pl.pallas_call(
        near_kernel,
        out_shape=jax.ShapeDtypeStruct((2, 2 * block, 2 * block), F32),
        in_specs=in_vmem(3),
        out_specs=in_vmem(1)[0],
        scratch_shapes=[pltpu.VMEM((4 * block, leaf), BF16)],
        compiler_params=params,
        cost_estimate=pl.CostEstimate(flops=20 << 30, bytes_accessed=16 << 20, transcendentals=0),
        name="near_columns",
    )(l_all, weights, k_core)
    k_diag = to_core(k_x)
    between = pl.pallas_call(
        far_kernel,
        out_shape=jax.ShapeDtypeStruct((2, 2, block, full), BF16),
        in_specs=in_vmem(5),
        out_specs=in_vmem(1)[0],
        scratch_shapes=[pltpu.VMEM((4 * block, leaf), BF16)],
        compiler_params=params,
        name="far_columns",
    )(near, keep, l_all, k_x, k_diag)
    packed = pl.pallas_call(
        pack_kernel,
        out_shape=jax.ShapeDtypeStruct((2, 4, block, angles), BF16),
        in_specs=in_vmem(4),
        out_specs=in_vmem(1)[0],
        compiler_params=params,
        name="pack_rows",
    )(kept_partial, partial_x, keep, between)
    folded = pl.pallas_call(
        functools.partial(fold_kernel, share),
        out_shape=jax.ShapeDtypeStruct((2 * share, 2 * full), BF16),
        in_specs=in_vmem(4),
        out_specs=in_vmem(1)[0],
        scratch_shapes=[pltpu.VMEM((2, 2 * share, full), F32)],
        compiler_params=params,
        name="fold_coupling",
    )(weights, k_x, k_core, k_diag)
    held = {0: packed}
    for j in range(1, clusters):
        pairs = [
            (4 * i + row, 4 * ROUNDS[row % 2][j][i] + row) for i in range(clusters) for row in range(4)
        ]
        held[j] = lax.ppermute(packed, ("clus", "rows"), pairs)
    pieces = []
    for j in range(clusters):
        pieces += [held[j], to_core(held[j])]
    field = pl.pallas_call(
        functools.partial(chain_kernel, clusters, quarter),
        out_shape=jax.ShapeDtypeStruct((2 * share, angles), BF16),
        in_specs=in_vmem(2 * clusters + 1),
        out_specs=in_vmem(1)[0],
        scratch_shapes=[
            pltpu.VMEM((clusters, full, 2 * full), BF16),
            pltpu.VMEM((clusters, full, 2 * angles), F32),
            pltpu.VMEM((clusters, 2 * full, 2 * angles), BF16),
        ],
        compiler_params=params,
        name="skeleton_chain",
    )(*pieces, folded)
    return field.reshape(share, 2, angles)


def body(excitation, leaf_factor, coupling, ranks):
    clusters, quarter, leaf = leaf_factor.shape[2:]
    share, _, angles = excitation.shape
    rows = lax.axis_size("rows")
    full = rows * clusters * quarter
    gathered = 4 * clusters * full * (angles + full)
    fits = (
        rows == 4
        and clusters == lax.axis_size("clus")
        and clusters == len(ROUNDS[0])
        and quarter == 8
        and angles == full == 128
        and share * rows == leaf
        and gathered <= SMALL_GATHER
    )
    plan = gather_body if fits else step_body
    return plan(excitation, leaf_factor, coupling, ranks)


def solution(mesh):
    placed = (
        P(("freq", "clus", "rows"), None, None),
        P("freq", "clus", None, "rows", None),
        P("freq", "clus", None, "rows", None),
        P("freq", None),
    )
    return jax.shard_map(
        body,
        mesh=mesh,
        in_specs=placed,
        out_specs=P(("freq", "clus", "rows"), None, None),
        check_vma=False,
    )
```

```python
import functools

import jax
import jax.numpy as jnp
from jax import lax
from jax.experimental import pallas as pl
from jax.experimental.pallas import tpu as pltpu
from jax.sharding import PartitionSpec as P

STEPS = 3
F32 = jnp.float32
BF16 = jnp.bfloat16
SMALL_GATHER = 4 << 20
ROUNDS = (
    ((0, 1, 2, 3), (2, 0, 3, 1), (1, 3, 0, 2), (3, 2, 1, 0)),
    ((0, 1, 2, 3), (3, 0, 1, 2), (1, 2, 3, 0), (2, 3, 0, 1)),
)


def complex_dot(a_real, a_imag, b_real, b_imag):
    real_part = jnp.dot(a_real, b_real, preferred_element_type=F32) - jnp.dot(
        a_imag, b_imag, preferred_element_type=F32
    )
    imag_part = jnp.dot(a_real, b_imag, preferred_element_type=F32) + jnp.dot(
        a_imag, b_real, preferred_element_type=F32
    )
    return (real_part, imag_part)


def transposed_dot(columns, skel_flat):
    real_part = jnp.einsum(
        "km,kr->mr", columns[0], skel_flat[0], preferred_element_type=F32
    ) - jnp.einsum("km,kr->mr", columns[1], skel_flat[1], preferred_element_type=F32)
    imag_part = jnp.einsum(
        "km,kr->mr", columns[0], skel_flat[1], preferred_element_type=F32
    ) + jnp.einsum("km,kr->mr", columns[1], skel_flat[0], preferred_element_type=F32)
    return jnp.stack([real_part, imag_part], axis=1)


def apply_once(current, factor, weights, keep_mask, clusters, quarter, leaf_size, angles, part_row):
    gathered = lax.all_gather(current, "rows", axis=0, tiled=True)
    real_part, imag_part = complex_dot(factor[0], factor[1], gathered[:, 0], gathered[:, 1])
    skeleton = jnp.stack([real_part, imag_part]).astype(BF16).reshape(2, clusters, quarter, angles)
    received = lax.all_to_all(skeleton, "clus", split_axis=1, concat_axis=1, tiled=True)
    received = received * keep_mask[None, :, :, None]
    skel_flat = received.reshape(2, clusters * quarter, angles)
    share_rows = leaf_size // lax.axis_size("rows")
    partial_sum = transposed_dot(weights, skel_flat)
    summed = lax.psum(partial_sum, "rows")
    own_rows = lax.dynamic_slice_in_dim(summed, part_row * share_rows, share_rows, 0)
    return own_rows.astype(BF16)


def step_body(excitation, leaf_factor, coupling, ranks):
    cluster = lax.axis_index("clus")
    part_row = lax.axis_index("rows")
    clusters = leaf_factor.shape[2]
    quarter = leaf_factor.shape[3]
    leaf_size = leaf_factor.shape[4]
    angles = excitation.shape[2]
    factor = leaf_factor.reshape(2, clusters * quarter, leaf_size)
    weights = coupling.reshape(2, clusters * quarter, leaf_size)
    rank_row = lax.dynamic_slice_in_dim(ranks, cluster, 1, 0)[0]
    rank_level = part_row * quarter + jnp.arange(quarter, dtype=jnp.int32)
    keep_mask = (rank_level[None, :] < rank_row[:, None]).astype(BF16)
    current = excitation
    for step in range(STEPS):
        current = apply_once(
            current, factor, weights, keep_mask, clusters, quarter, leaf_size, angles, part_row
        )
    return current


def combine(product, rows, columns):
    real_part = product[:rows, :columns] - product[rows:, columns:]
    imag_part = product[:rows, columns:] + product[rows:, :columns]
    return real_part, imag_part


def load_kernel(
    share, angles, quarter, ranks, l_hbm, x_hbm, x_near,
    l_own, x_own, x_core, keep, x_flat, x_wide, sems,
):
    copies = [
        pltpu.make_async_copy(source, target, sems.at[i])
        for i, (source, target) in enumerate(((x_hbm, x_flat), (l_hbm, l_own)))
    ]
    for copy in copies:
        copy.start()
    row = lax.axis_index("rows")
    cluster = lax.axis_index("clus")
    level = lax.broadcasted_iota(jnp.int32, (quarter, angles), 0)
    for at, flip in enumerate((0, 2, 1, 3)):
        base = (row ^ flip) * quarter
        for target in range(keep.shape[1] // quarter):
            below = level + base < ranks[target, cluster]
            keep[at, target * quarter : (target + 1) * quarter, :] = below.astype(F32)
    copies[0].wait()
    for source, target in ((x_flat, x_own), (x_near, x_core)):
        x_wide[...] = source[...].astype(F32)
        for part in range(2):
            target[:, part * angles : (part + 1) * angles] = x_wide[
                pl.ds(part, share, stride=2), :
            ].astype(BF16)
    copies[1].wait()


def side_kernel(share, angles, l_own, l_x, x_own, x_core, partial, kept_partial, l_all):
    row = lax.axis_index("rows")
    block = l_own.shape[1]
    for part in range(2):
        for at, ref in enumerate((l_own, l_x)):
            first = (2 * part + at) * block
            l_all[first : first + block, :] = ref[part]
    total = None
    for ref, quarter in ((x_own, row), (x_core, row ^ 1)):
        columns = l_all[:, pl.ds(pl.multiple_of(quarter * share, share), share)]
        term = jnp.dot(columns, ref[...], preferred_element_type=F32)
        total = term if total is None else total + term
    for part, value in enumerate(combine(total, 2 * block, angles)):
        for at in range(2):
            rows = value[at * block : (at + 1) * block]
            kept_partial[at, part] = rows
            partial[at, part] = rows.astype(BF16)


def operator_columns(l_all, k_refs, k_rows):
    block = k_refs[0].shape[1]
    for part in range(2):
        for at, ref in enumerate(k_refs):
            first = (2 * part + at) * block
            k_rows[first : first + block, :] = ref[part]
    product = lax.dot_general(
        l_all[...], k_rows[...], (((1,), (1,)), ((), ())), preferred_element_type=F32
    )
    return combine(product, 2 * block, 2 * block)


def near_kernel(l_all, k_own, k_core, near, k_rows):
    near[0], near[1] = operator_columns(l_all, (k_own, k_core), k_rows)


def far_kernel(near, keep, l_all, k_x, k_diag, between, k_rows):
    block = keep.shape[1]
    for part, far in enumerate(operator_columns(l_all, (k_x, k_diag), k_rows)):
        value = near[part]
        columns = [value[:, :block], far[:, :block], value[:, block:], far[:, block:]]
        value = jnp.concatenate(columns, axis=1)
        odd = lax.axis_index("rows") % 2 == 1
        value = jnp.where(odd, pltpu.roll(value, 2 * block, 1), value)
        for at in range(2):
            between[at, part] = (value[at * block : (at + 1) * block] * keep[at]).astype(BF16)


def pack_kernel(partial, partial_x, keep, between, packed):
    for at in range(2):
        for part in range(2):
            value = partial[at, part] + partial_x[1 - at, part].astype(F32)
            packed[at, part] = (value * keep[at]).astype(BF16)
            packed[at, 2 + part] = between[at, part]


def fold_kernel(share, k_own, k_x, k_core, k_diag, folded, wide):
    row = lax.axis_index("rows")
    mine = pl.ds(pl.multiple_of(row * share, share), share)
    odd = row % 2 == 1
    near, far = (k_own, k_x), (k_core, k_diag)
    real, imag = (
        jnp.concatenate(
            [
                jnp.where(odd, b[part, :, mine].astype(F32), a[part, :, mine].astype(F32))
                for first, second in ((near, far), (far, near))
                for a, b in zip(first, second, strict=True)
            ],
            axis=0,
        ).T
        for part in range(2)
    )
    full = real.shape[1]
    even, odd = pl.ds(0, share, stride=2), pl.ds(1, share, stride=2)
    wide[0, even, :] = real
    wide[1, even, :] = -imag
    wide[0, odd, :] = imag
    wide[1, odd, :] = real
    folded[:, :full] = wide[0].astype(BF16)
    folded[:, full:] = wide[1].astype(BF16)


def sender(targets, cluster):
    source = jnp.int32(0)
    for at, target in enumerate(targets):
        source = jnp.where(cluster == target, at, source)
    return source


def chain_kernel(clusters, quarter, *refs):
    pieces, folded, field = refs[: 2 * clusters], refs[2 * clusters], refs[2 * clusters + 1]
    between, skeleton, kept = refs[2 * clusters + 2 :]
    row = lax.axis_index("rows")
    cluster = lax.axis_index("clus")
    block = clusters * quarter
    full = 4 * block
    for j in range(clusters):
        senders = [sender(rounds[j], cluster) for rounds in ROUNDS]
        for core in range(2):
            source = jnp.where(row % 2 == core, senders[0], senders[1])
            ref = pieces[2 * j + core]
            for at in range(2):
                first = ((row % 2) ^ core) * 2 * block + at * block
                rows = pl.ds(pl.multiple_of(first, block), block)
                for part in range(2):
                    columns = slice(part * full, (part + 1) * full)
                    skeleton[source, rows, columns] = ref[at, part].astype(F32)
                    between[source, rows, columns] = ref[at, 2 + part]

    def gather(target):
        rows = [
            skeleton[s, pl.ds(pl.multiple_of(q * block + target * quarter, quarter), quarter), :]
            for q in range(4)
            for s in range(clusters)
        ]
        return jnp.concatenate(rows, axis=0)

    def embed(target, value):
        kept[target, :full, :] = value.astype(BF16)
        kept[target, full:, :full] = (-value[:, full:]).astype(BF16)
        kept[target, full:, full:] = value[:, :full].astype(BF16)

    def own_target(source):
        blocks = []
        for q in range(4):
            rows = between[source, q * block : (q + 1) * block, :].astype(F32)
            chosen = rows[:quarter]
            for target in range(1, clusters):
                other = rows[target * quarter : (target + 1) * quarter]
                chosen = jnp.where(cluster == target, other, chosen)
            blocks.append(chosen)
        return jnp.concatenate(blocks, axis=0).astype(BF16)

    for target in range(clusters):
        embed(target, gather(target))
    for step in range(STEPS - 2):
        for source in range(clusters):
            skeleton[source] = jnp.dot(between[source], kept[source], preferred_element_type=F32)
        for target in range(clusters):
            embed(target, gather(target))
    wanted = [
        jnp.dot(own_target(source), kept[source], preferred_element_type=F32)
        for source in range(clusters)
    ]
    value = jnp.concatenate(
        [wanted[s][q * quarter : (q + 1) * quarter] for q in range(4) for s in range(clusters)], axis=0
    )
    last = jnp.concatenate([value[:, :full], value[:, full:]], axis=0).astype(BF16)
    field[...] = jnp.dot(folded[...], last, preferred_element_type=F32).astype(BF16)


def in_vmem(count):
    return [pl.BlockSpec(memory_space=pltpu.VMEM)] * count


def gather_body(excitation, leaf_factor, coupling, ranks):
    clusters, quarter, leaf = leaf_factor.shape[2:]
    share, _, angles = excitation.shape
    block = clusters * quarter
    full = 4 * block
    params = pltpu.CompilerParams(vmem_limit_bytes=32 << 20)

    def across(flip):
        return lambda v: lax.ppermute(v, "rows", [(i, i ^ flip) for i in range(4)])

    to_x, to_core = across(2), across(1)
    factor = leaf_factor.reshape(2, block, leaf)
    weights = coupling.reshape(2, block, leaf)
    l_x = to_x(factor)
    current = excitation.reshape(2 * share, angles)
    x_near = to_core(current)
    to_send, _ = lax.optimization_barrier((weights, x_near))
    k_x = to_x(to_send)
    k_core = to_core(weights)
    l_own, x_own, x_core, keep = pl.pallas_call(
        functools.partial(load_kernel, share, angles, quarter),
        out_shape=(
            jax.ShapeDtypeStruct(factor.shape, BF16),
            jax.ShapeDtypeStruct((share, 2 * angles), BF16),
            jax.ShapeDtypeStruct((share, 2 * angles), BF16),
            jax.ShapeDtypeStruct((4, block, angles), F32),
        ),
        in_specs=[pl.BlockSpec(memory_space=pltpu.SMEM)]
        + [pl.BlockSpec(memory_space=pl.ANY)] * 2
        + in_vmem(1),
        out_specs=tuple(in_vmem(4)),
        scratch_shapes=[
            pltpu.VMEM((2 * share, angles), BF16),
            pltpu.VMEM((2 * share, angles), F32),
            pltpu.SemaphoreType.DMA((2,)),
        ],
        compiler_params=params,
        name="load_own",
    )(ranks, factor, current, x_near)
    partial, kept_partial, l_all = pl.pallas_call(
        functools.partial(side_kernel, share, angles),
        out_shape=(
            jax.ShapeDtypeStruct((2, 2, block, angles), BF16),
            jax.ShapeDtypeStruct((2, 2, block, angles), F32),
            jax.ShapeDtypeStruct((4 * block, leaf), BF16),
        ),
        in_specs=in_vmem(4),
        out_specs=tuple(in_vmem(3)),
        compiler_params=params,
        cost_estimate=pl.CostEstimate(flops=1 << 30, bytes_accessed=16 << 20, transcendentals=0),
        name="side_skeleton",
    )(l_own, l_x, x_own, x_core)
    partial_x = to_x(partial)
    near = pl.pallas_call(
        near_kernel,
        out_shape=jax.ShapeDtypeStruct((2, 2 * block, 2 * block), F32),
        in_specs=in_vmem(3),
        out_specs=in_vmem(1)[0],
        scratch_shapes=[pltpu.VMEM((4 * block, leaf), BF16)],
        compiler_params=params,
        cost_estimate=pl.CostEstimate(flops=20 << 30, bytes_accessed=16 << 20, transcendentals=0),
        name="near_columns",
    )(l_all, weights, k_core)
    k_diag = to_core(k_x)
    between = pl.pallas_call(
        far_kernel,
        out_shape=jax.ShapeDtypeStruct((2, 2, block, full), BF16),
        in_specs=in_vmem(5),
        out_specs=in_vmem(1)[0],
        scratch_shapes=[pltpu.VMEM((4 * block, leaf), BF16)],
        compiler_params=params,
        name="far_columns",
    )(near, keep, l_all, k_x, k_diag)
    packed = pl.pallas_call(
        pack_kernel,
        out_shape=jax.ShapeDtypeStruct((2, 4, block, angles), BF16),
        in_specs=in_vmem(4),
        out_specs=in_vmem(1)[0],
        compiler_params=params,
        name="pack_rows",
    )(kept_partial, partial_x, keep, between)
    folded = pl.pallas_call(
        functools.partial(fold_kernel, share),
        out_shape=jax.ShapeDtypeStruct((2 * share, 2 * full), BF16),
        in_specs=in_vmem(4),
        out_specs=in_vmem(1)[0],
        scratch_shapes=[pltpu.VMEM((2, 2 * share, full), F32)],
        compiler_params=params,
        name="fold_coupling",
    )(weights, k_x, k_core, k_diag)
    held = {0: packed}
    for j in range(1, clusters):
        pairs = [
            (4 * i + row, 4 * ROUNDS[row % 2][j][i] + row) for i in range(clusters) for row in range(4)
        ]
        held[j] = lax.ppermute(packed, ("clus", "rows"), pairs)
    pieces = []
    for j in range(clusters):
        pieces += [held[j], to_core(held[j])]
    field = pl.pallas_call(
        functools.partial(chain_kernel, clusters, quarter),
        out_shape=jax.ShapeDtypeStruct((2 * share, angles), BF16),
        in_specs=in_vmem(2 * clusters + 1),
        out_specs=in_vmem(1)[0],
        scratch_shapes=[
            pltpu.VMEM((clusters, full, 2 * full), BF16),
            pltpu.VMEM((clusters, full, 2 * angles), F32),
            pltpu.VMEM((clusters, 2 * full, 2 * angles), BF16),
        ],
        compiler_params=params,
        name="skeleton_chain",
    )(*pieces, folded)
    return field.reshape(share, 2, angles)


def body(excitation, leaf_factor, coupling, ranks):
    clusters, quarter, leaf = leaf_factor.shape[2:]
    share, _, angles = excitation.shape
    rows = lax.axis_size("rows")
    full = rows * clusters * quarter
    gathered = 4 * clusters * full * (angles + full)
    fits = (
        rows == 4
        and clusters == lax.axis_size("clus")
        and clusters == len(ROUNDS[0])
        and quarter == 8
        and angles == full == 128
        and share * rows == leaf
        and gathered <= SMALL_GATHER
    )
    plan = gather_body if fits else step_body
    return plan(excitation, leaf_factor, coupling, ranks)


def solution(mesh):
    placed = (
        P(("freq", "clus", "rows"), None, None),
        P("freq", "clus", None, "rows", None),
        P("freq", "clus", None, "rows", None),
        P("freq", None),
    )
    return jax.shard_map(
        body,
        mesh=mesh,
        in_specs=placed,
        out_specs=P(("freq", "clus", "rows"), None, None),
        check_vma=False,
    )
```

```python
import functools

import jax
import jax.numpy as jnp
from jax import lax
from jax.experimental import pallas as pl
from jax.experimental.pallas import tpu as pltpu
from jax.sharding import PartitionSpec as P

STEPS = 3
F32 = jnp.float32
BF16 = jnp.bfloat16
SMALL_GATHER = 4 << 20
ROUNDS = (
    ((0, 1, 2, 3), (2, 0, 3, 1), (1, 3, 0, 2), (3, 2, 1, 0)),
    ((0, 1, 2, 3), (3, 0, 1, 2), (1, 2, 3, 0), (2, 3, 0, 1)),
)


def complex_dot(a_real, a_imag, b_real, b_imag):
    real_part = jnp.dot(a_real, b_real, preferred_element_type=F32) - jnp.dot(
        a_imag, b_imag, preferred_element_type=F32
    )
    imag_part = jnp.dot(a_real, b_imag, preferred_element_type=F32) + jnp.dot(
        a_imag, b_real, preferred_element_type=F32
    )
    return (real_part, imag_part)


def transposed_dot(columns, skel_flat):
    real_part = jnp.einsum(
        "km,kr->mr", columns[0], skel_flat[0], preferred_element_type=F32
    ) - jnp.einsum("km,kr->mr", columns[1], skel_flat[1], preferred_element_type=F32)
    imag_part = jnp.einsum(
        "km,kr->mr", columns[0], skel_flat[1], preferred_element_type=F32
    ) + jnp.einsum("km,kr->mr", columns[1], skel_flat[0], preferred_element_type=F32)
    return jnp.stack([real_part, imag_part], axis=1)


def apply_once(current, factor, weights, keep_mask, clusters, quarter, leaf_size, angles, part_row):
    gathered = lax.all_gather(current, "rows", axis=0, tiled=True)
    real_part, imag_part = complex_dot(factor[0], factor[1], gathered[:, 0], gathered[:, 1])
    skeleton = jnp.stack([real_part, imag_part]).astype(BF16).reshape(2, clusters, quarter, angles)
    received = lax.all_to_all(skeleton, "clus", split_axis=1, concat_axis=1, tiled=True)
    received = received * keep_mask[None, :, :, None]
    skel_flat = received.reshape(2, clusters * quarter, angles)
    share_rows = leaf_size // lax.axis_size("rows")
    partial_sum = transposed_dot(weights, skel_flat)
    summed = lax.psum(partial_sum, "rows")
    own_rows = lax.dynamic_slice_in_dim(summed, part_row * share_rows, share_rows, 0)
    return own_rows.astype(BF16)


def step_body(excitation, leaf_factor, coupling, ranks):
    cluster = lax.axis_index("clus")
    part_row = lax.axis_index("rows")
    clusters = leaf_factor.shape[2]
    quarter = leaf_factor.shape[3]
    leaf_size = leaf_factor.shape[4]
    angles = excitation.shape[2]
    factor = leaf_factor.reshape(2, clusters * quarter, leaf_size)
    weights = coupling.reshape(2, clusters * quarter, leaf_size)
    rank_row = lax.dynamic_slice_in_dim(ranks, cluster, 1, 0)[0]
    rank_level = part_row * quarter + jnp.arange(quarter, dtype=jnp.int32)
    keep_mask = (rank_level[None, :] < rank_row[:, None]).astype(BF16)
    current = excitation
    for step in range(STEPS):
        current = apply_once(
            current, factor, weights, keep_mask, clusters, quarter, leaf_size, angles, part_row
        )
    return current


def combine(product, rows, columns):
    real_part = product[:rows, :columns] - product[rows:, columns:]
    imag_part = product[:rows, columns:] + product[rows:, :columns]
    return real_part, imag_part


def load_kernel(
    share, angles, quarter, ranks, l_hbm, x_hbm, x_near,
    l_own, x_own, x_core, keep, x_flat, x_wide, sems,
):
    copies = [
        pltpu.make_async_copy(source, target, sems.at[i])
        for i, (source, target) in enumerate(((x_hbm, x_flat), (l_hbm, l_own)))
    ]
    for copy in copies:
        copy.start()
    row = lax.axis_index("rows")
    cluster = lax.axis_index("clus")
    level = lax.broadcasted_iota(jnp.int32, (quarter, angles), 0)
    for at, flip in enumerate((0, 2, 1, 3)):
        base = (row ^ flip) * quarter
        for target in range(keep.shape[1] // quarter):
            below = level + base < ranks[target, cluster]
            keep[at, target * quarter : (target + 1) * quarter, :] = below.astype(F32)
    copies[0].wait()
    for source, target in ((x_flat, x_own), (x_near, x_core)):
        x_wide[...] = source[...].astype(F32)
        for part in range(2):
            target[:, part * angles : (part + 1) * angles] = x_wide[
                pl.ds(part, share, stride=2), :
            ].astype(BF16)
    copies[1].wait()


def side_kernel(share, angles, l_own, l_x, x_own, x_core, partial, kept_partial, l_all):
    row = lax.axis_index("rows")
    block = l_own.shape[1]
    for part in range(2):
        for at, ref in enumerate((l_own, l_x)):
            first = (2 * part + at) * block
            l_all[first : first + block, :] = ref[part]
    total = None
    for ref, quarter in ((x_own, row), (x_core, row ^ 1)):
        columns = l_all[:, pl.ds(pl.multiple_of(quarter * share, share), share)]
        term = jnp.dot(columns, ref[...], preferred_element_type=F32)
        total = term if total is None else total + term
    for part, value in enumerate(combine(total, 2 * block, angles)):
        for at in range(2):
            rows = value[at * block : (at + 1) * block]
            kept_partial[at, part] = rows
            partial[at, part] = rows.astype(BF16)


def operator_columns(l_all, k_refs, k_rows):
    block = k_refs[0].shape[1]
    for part in range(2):
        for at, ref in enumerate(k_refs):
            first = (2 * part + at) * block
            k_rows[first : first + block, :] = ref[part]
    product = lax.dot_general(
        l_all[...], k_rows[...], (((1,), (1,)), ((), ())), preferred_element_type=F32
    )
    return combine(product, 2 * block, 2 * block)


def near_kernel(l_all, k_own, k_core, near, k_rows):
    near[0], near[1] = operator_columns(l_all, (k_own, k_core), k_rows)


def far_kernel(near, keep, l_all, k_x, k_diag, between, k_rows):
    block = keep.shape[1]
    for part, far in enumerate(operator_columns(l_all, (k_x, k_diag), k_rows)):
        value = near[part]
        columns = [value[:, :block], far[:, :block], value[:, block:], far[:, block:]]
        value = jnp.concatenate(columns, axis=1)
        odd = lax.axis_index("rows") % 2 == 1
        value = jnp.where(odd, pltpu.roll(value, 2 * block, 1), value)
        for at in range(2):
            between[at, 2 + part] = (value[at * block : (at + 1) * block] * keep[at]).astype(BF16)


def pack_kernel(partial, partial_x, keep, between, packed):
    for at in range(2):
        for part in range(2):
            value = partial[at, part] + partial_x[1 - at, part].astype(F32)
            packed[at, part] = (value * keep[at]).astype(BF16)


def fold_kernel(share, k_own, k_x, k_core, k_diag, folded, wide):
    row = lax.axis_index("rows")
    mine = pl.ds(pl.multiple_of(row * share, share), share)
    odd = row % 2 == 1
    near, far = (k_own, k_x), (k_core, k_diag)
    real, imag = (
        jnp.concatenate(
            [
                jnp.where(odd, b[part, :, mine].astype(F32), a[part, :, mine].astype(F32))
                for first, second in ((near, far), (far, near))
                for a, b in zip(first, second, strict=True)
            ],
            axis=0,
        ).T
        for part in range(2)
    )
    full = real.shape[1]
    even, odd = pl.ds(0, share, stride=2), pl.ds(1, share, stride=2)
    wide[0, even, :] = real
    wide[1, even, :] = -imag
    wide[0, odd, :] = imag
    wide[1, odd, :] = real
    folded[:, :full] = wide[0].astype(BF16)
    folded[:, full:] = wide[1].astype(BF16)


def sender(targets, cluster):
    source = jnp.int32(0)
    for at, target in enumerate(targets):
        source = jnp.where(cluster == target, at, source)
    return source


def chain_kernel(clusters, quarter, *refs):
    pieces, folded, field = refs[: 2 * clusters], refs[2 * clusters], refs[2 * clusters + 1]
    between, skeleton, kept = refs[2 * clusters + 2 :]
    row = lax.axis_index("rows")
    cluster = lax.axis_index("clus")
    block = clusters * quarter
    full = 4 * block
    for j in range(clusters):
        senders = [sender(rounds[j], cluster) for rounds in ROUNDS]
        for core in range(2):
            source = jnp.where(row % 2 == core, senders[0], senders[1])
            ref = pieces[2 * j + core]
            for at in range(2):
                first = ((row % 2) ^ core) * 2 * block + at * block
                rows = pl.ds(pl.multiple_of(first, block), block)
                for part in range(2):
                    columns = slice(part * full, (part + 1) * full)
                    skeleton[source, rows, columns] = ref[at, part].astype(F32)
                    between[source, rows, columns] = ref[at, 2 + part]

    def gather(target):
        rows = [
            skeleton[s, pl.ds(pl.multiple_of(q * block + target * quarter, quarter), quarter), :]
            for q in range(4)
            for s in range(clusters)
        ]
        return jnp.concatenate(rows, axis=0)

    def embed(target, value):
        kept[target, :full, :] = value.astype(BF16)
        kept[target, full:, :full] = (-value[:, full:]).astype(BF16)
        kept[target, full:, full:] = value[:, :full].astype(BF16)

    def own_target(source):
        blocks = []
        for q in range(4):
            rows = between[source, q * block : (q + 1) * block, :].astype(F32)
            chosen = rows[:quarter]
            for target in range(1, clusters):
                other = rows[target * quarter : (target + 1) * quarter]
                chosen = jnp.where(cluster == target, other, chosen)
            blocks.append(chosen)
        return jnp.concatenate(blocks, axis=0).astype(BF16)

    for target in range(clusters):
        embed(target, gather(target))
    for step in range(STEPS - 2):
        for source in range(clusters):
            skeleton[source] = jnp.dot(between[source], kept[source], preferred_element_type=F32)
        for target in range(clusters):
            embed(target, gather(target))
    wanted = [
        jnp.dot(own_target(source), kept[source], preferred_element_type=F32)
        for source in range(clusters)
    ]
    value = jnp.concatenate(
        [wanted[s][q * quarter : (q + 1) * quarter] for q in range(4) for s in range(clusters)], axis=0
    )
    last = jnp.concatenate([value[:, :full], value[:, full:]], axis=0).astype(BF16)
    field[...] = jnp.dot(folded[...], last, preferred_element_type=F32).astype(BF16)


def in_vmem(count):
    return [pl.BlockSpec(memory_space=pltpu.VMEM)] * count


def gather_body(excitation, leaf_factor, coupling, ranks):
    clusters, quarter, leaf = leaf_factor.shape[2:]
    share, _, angles = excitation.shape
    block = clusters * quarter
    full = 4 * block
    params = pltpu.CompilerParams(vmem_limit_bytes=32 << 20)

    def across(flip):
        return lambda v: lax.ppermute(v, "rows", [(i, i ^ flip) for i in range(4)])

    to_x, to_core = across(2), across(1)
    factor = leaf_factor.reshape(2, block, leaf)
    weights = coupling.reshape(2, block, leaf)
    l_x = to_x(factor)
    current = excitation.reshape(2 * share, angles)
    x_near = to_core(current)
    to_send, _ = lax.optimization_barrier((weights, x_near))
    k_x = to_x(to_send)
    k_core = to_core(weights)
    l_own, x_own, x_core, keep = pl.pallas_call(
        functools.partial(load_kernel, share, angles, quarter),
        out_shape=(
            jax.ShapeDtypeStruct(factor.shape, BF16),
            jax.ShapeDtypeStruct((share, 2 * angles), BF16),
            jax.ShapeDtypeStruct((share, 2 * angles), BF16),
            jax.ShapeDtypeStruct((4, block, angles), F32),
        ),
        in_specs=[pl.BlockSpec(memory_space=pltpu.SMEM)]
        + [pl.BlockSpec(memory_space=pl.ANY)] * 2
        + in_vmem(1),
        out_specs=tuple(in_vmem(4)),
        scratch_shapes=[
            pltpu.VMEM((2 * share, angles), BF16),
            pltpu.VMEM((2 * share, angles), F32),
            pltpu.SemaphoreType.DMA((2,)),
        ],
        compiler_params=params,
        name="load_own",
    )(ranks, factor, current, x_near)
    partial, kept_partial, l_all = pl.pallas_call(
        functools.partial(side_kernel, share, angles),
        out_shape=(
            jax.ShapeDtypeStruct((2, 2, block, angles), BF16),
            jax.ShapeDtypeStruct((2, 2, block, angles), F32),
            jax.ShapeDtypeStruct((4 * block, leaf), BF16),
        ),
        in_specs=in_vmem(4),
        out_specs=tuple(in_vmem(3)),
        compiler_params=params,
        cost_estimate=pl.CostEstimate(flops=1 << 30, bytes_accessed=16 << 20, transcendentals=0),
        name="side_skeleton",
    )(l_own, l_x, x_own, x_core)
    partial_x = to_x(partial)
    near = pl.pallas_call(
        near_kernel,
        out_shape=jax.ShapeDtypeStruct((2, 2 * block, 2 * block), F32),
        in_specs=in_vmem(3),
        out_specs=in_vmem(1)[0],
        scratch_shapes=[pltpu.VMEM((4 * block, leaf), BF16)],
        compiler_params=params,
        cost_estimate=pl.CostEstimate(flops=20 << 30, bytes_accessed=16 << 20, transcendentals=0),
        name="near_columns",
    )(l_all, weights, k_core)
    k_diag = to_core(k_x)
    between = pl.pallas_call(
        far_kernel,
        out_shape=jax.ShapeDtypeStruct((2, 4, block, full), BF16),
        in_specs=in_vmem(5),
        out_specs=in_vmem(1)[0],
        scratch_shapes=[pltpu.VMEM((4 * block, leaf), BF16)],
        compiler_params=params,
        name="far_columns",
    )(near, keep, l_all, k_x, k_diag)
    packed = pl.pallas_call(
        pack_kernel,
        out_shape=jax.ShapeDtypeStruct((2, 4, block, angles), BF16),
        in_specs=in_vmem(4),
        out_specs=in_vmem(1)[0],
        input_output_aliases={3: 0},
        compiler_params=params,
        name="pack_rows",
    )(kept_partial, partial_x, keep, between)
    folded = pl.pallas_call(
        functools.partial(fold_kernel, share),
        out_shape=jax.ShapeDtypeStruct((2 * share, 2 * full), BF16),
        in_specs=in_vmem(4),
        out_specs=in_vmem(1)[0],
        scratch_shapes=[pltpu.VMEM((2, 2 * share, full), F32)],
        compiler_params=params,
        name="fold_coupling",
    )(weights, k_x, k_core, k_diag)
    held = {0: packed}
    for j in range(1, clusters):
        pairs = [
            (4 * i + row, 4 * ROUNDS[row % 2][j][i] + row) for i in range(clusters) for row in range(4)
        ]
        held[j] = lax.ppermute(packed, ("clus", "rows"), pairs)
    pieces = []
    for j in range(clusters):
        pieces += [held[j], to_core(held[j])]
    field = pl.pallas_call(
        functools.partial(chain_kernel, clusters, quarter),
        out_shape=jax.ShapeDtypeStruct((2 * share, angles), BF16),
        in_specs=in_vmem(2 * clusters + 1),
        out_specs=in_vmem(1)[0],
        scratch_shapes=[
            pltpu.VMEM((clusters, full, 2 * full), BF16),
            pltpu.VMEM((clusters, full, 2 * angles), F32),
            pltpu.VMEM((clusters, 2 * full, 2 * angles), BF16),
        ],
        compiler_params=params,
        name="skeleton_chain",
    )(*pieces, folded)
    return field.reshape(share, 2, angles)


def body(excitation, leaf_factor, coupling, ranks):
    clusters, quarter, leaf = leaf_factor.shape[2:]
    share, _, angles = excitation.shape
    rows = lax.axis_size("rows")
    full = rows * clusters * quarter
    gathered = 4 * clusters * full * (angles + full)
    fits = (
        rows == 4
        and clusters == lax.axis_size("clus")
        and clusters == len(ROUNDS[0])
        and quarter == 8
        and angles == full == 128
        and share * rows == leaf
        and gathered <= SMALL_GATHER
    )
    plan = gather_body if fits else step_body
    return plan(excitation, leaf_factor, coupling, ranks)


def solution(mesh):
    placed = (
        P(("freq", "clus", "rows"), None, None),
        P("freq", "clus", None, "rows", None),
        P("freq", "clus", None, "rows", None),
        P("freq", None),
    )
    return jax.shard_map(
        body,
        mesh=mesh,
        in_specs=placed,
        out_specs=P(("freq", "clus", "rows"), None, None),
        check_vma=False,
    )
```

```python
import functools

import jax
import jax.numpy as jnp
from jax import lax
from jax.experimental import pallas as pl
from jax.experimental.pallas import tpu as pltpu
from jax.sharding import PartitionSpec as P

STEPS = 3
F32 = jnp.float32
BF16 = jnp.bfloat16
SMALL_GATHER = 4 << 20
ROUNDS = (
    ((0, 1, 2, 3), (2, 0, 3, 1), (1, 3, 0, 2), (3, 2, 1, 0)),
    ((0, 1, 2, 3), (3, 0, 1, 2), (1, 2, 3, 0), (2, 3, 0, 1)),
)


def complex_dot(a_real, a_imag, b_real, b_imag):
    real_part = jnp.dot(a_real, b_real, preferred_element_type=F32) - jnp.dot(
        a_imag, b_imag, preferred_element_type=F32
    )
    imag_part = jnp.dot(a_real, b_imag, preferred_element_type=F32) + jnp.dot(
        a_imag, b_real, preferred_element_type=F32
    )
    return (real_part, imag_part)


def transposed_dot(columns, skel_flat):
    real_part = jnp.einsum(
        "km,kr->mr", columns[0], skel_flat[0], preferred_element_type=F32
    ) - jnp.einsum("km,kr->mr", columns[1], skel_flat[1], preferred_element_type=F32)
    imag_part = jnp.einsum(
        "km,kr->mr", columns[0], skel_flat[1], preferred_element_type=F32
    ) + jnp.einsum("km,kr->mr", columns[1], skel_flat[0], preferred_element_type=F32)
    return jnp.stack([real_part, imag_part], axis=1)


def apply_once(current, factor, weights, keep_mask, clusters, quarter, leaf_size, angles, part_row):
    gathered = lax.all_gather(current, "rows", axis=0, tiled=True)
    real_part, imag_part = complex_dot(factor[0], factor[1], gathered[:, 0], gathered[:, 1])
    skeleton = jnp.stack([real_part, imag_part]).astype(BF16).reshape(2, clusters, quarter, angles)
    received = lax.all_to_all(skeleton, "clus", split_axis=1, concat_axis=1, tiled=True)
    received = received * keep_mask[None, :, :, None]
    skel_flat = received.reshape(2, clusters * quarter, angles)
    share_rows = leaf_size // lax.axis_size("rows")
    partial_sum = transposed_dot(weights, skel_flat)
    summed = lax.psum(partial_sum, "rows")
    own_rows = lax.dynamic_slice_in_dim(summed, part_row * share_rows, share_rows, 0)
    return own_rows.astype(BF16)


def step_body(excitation, leaf_factor, coupling, ranks):
    cluster = lax.axis_index("clus")
    part_row = lax.axis_index("rows")
    clusters = leaf_factor.shape[2]
    quarter = leaf_factor.shape[3]
    leaf_size = leaf_factor.shape[4]
    angles = excitation.shape[2]
    factor = leaf_factor.reshape(2, clusters * quarter, leaf_size)
    weights = coupling.reshape(2, clusters * quarter, leaf_size)
    rank_row = lax.dynamic_slice_in_dim(ranks, cluster, 1, 0)[0]
    rank_level = part_row * quarter + jnp.arange(quarter, dtype=jnp.int32)
    keep_mask = (rank_level[None, :] < rank_row[:, None]).astype(BF16)
    current = excitation
    for step in range(STEPS):
        current = apply_once(
            current, factor, weights, keep_mask, clusters, quarter, leaf_size, angles, part_row
        )
    return current


def combine(product, rows, columns):
    real_part = product[:rows, :columns] - product[rows:, columns:]
    imag_part = product[:rows, columns:] + product[rows:, :columns]
    return real_part, imag_part


def load_kernel(
    share, angles, quarter, ranks, l_hbm, x_hbm, x_near,
    l_own, x_own, x_core, keep, x_flat, x_wide, sems,
):
    copies = [
        pltpu.make_async_copy(source, target, sems.at[i])
        for i, (source, target) in enumerate(((x_hbm, x_flat), (l_hbm, l_own)))
    ]
    for copy in copies:
        copy.start()
    row = lax.axis_index("rows")
    cluster = lax.axis_index("clus")
    level = lax.broadcasted_iota(jnp.int32, (quarter, angles), 0)
    for at, flip in enumerate((0, 2, 1, 3)):
        base = (row ^ flip) * quarter
        for target in range(keep.shape[1] // quarter):
            below = level + base < ranks[target, cluster]
            keep[at, target * quarter : (target + 1) * quarter, :] = below.astype(F32)
    copies[0].wait()
    for source, target in ((x_flat, x_own), (x_near, x_core)):
        x_wide[...] = source[...].astype(F32)
        for part in range(2):
            target[:, part * angles : (part + 1) * angles] = x_wide[
                pl.ds(part, share, stride=2), :
            ].astype(BF16)
    copies[1].wait()


def side_kernel(share, angles, l_own, l_x, x_own, x_core, partial, kept_partial, l_all):
    row = lax.axis_index("rows")
    block = l_own.shape[1]
    for part in range(2):
        for at, ref in enumerate((l_own, l_x)):
            first = (2 * part + at) * block
            l_all[first : first + block, :] = ref[part]
    total = None
    for ref, quarter in ((x_own, row), (x_core, row ^ 1)):
        columns = l_all[:, pl.ds(pl.multiple_of(quarter * share, share), share)]
        term = jnp.dot(columns, ref[...], preferred_element_type=F32)
        total = term if total is None else total + term
    for part, value in enumerate(combine(total, 2 * block, angles)):
        for at in range(2):
            rows = value[at * block : (at + 1) * block]
            kept_partial[at, part] = rows
            partial[at, part] = rows.astype(BF16)


def operator_columns(l_all, k_refs, k_rows):
    block = k_refs[0].shape[1]
    for part in range(2):
        for at, ref in enumerate(k_refs):
            first = (2 * part + at) * block
            k_rows[first : first + block, :] = ref[part]
    product = lax.dot_general(
        l_all[...], k_rows[...], (((1,), (1,)), ((), ())), preferred_element_type=F32
    )
    return combine(product, 2 * block, 2 * block)


def near_kernel(l_all, k_own, k_core, near, k_rows):
    near[0], near[1] = operator_columns(l_all, (k_own, k_core), k_rows)


def far_kernel(near, keep, l_all, k_x, k_diag, between, k_rows):
    block = keep.shape[1]
    for part, far in enumerate(operator_columns(l_all, (k_x, k_diag), k_rows)):
        value = near[part]
        columns = [value[:, :block], far[:, :block], value[:, block:], far[:, block:]]
        value = jnp.concatenate(columns, axis=1)
        odd = lax.axis_index("rows") % 2 == 1
        value = jnp.where(odd, pltpu.roll(value, 2 * block, 1), value)
        for at in range(2):
            between[at, part] = (value[at * block : (at + 1) * block] * keep[at]).astype(BF16)


def pack_kernel(partial, partial_x, keep, between, packed):
    for at in range(2):
        for part in range(2):
            value = partial[at, part] + partial_x[1 - at, part].astype(F32)
            packed[at, part] = (value * keep[at]).astype(BF16)
            packed[at, 2 + part] = between[at, part]


def fold_kernel(share, k_own, k_x, k_core, k_diag, folded, wide):
    row = lax.axis_index("rows")
    mine = pl.ds(pl.multiple_of(row * share, share), share)
    odd = row % 2 == 1
    near, far = (k_own, k_x), (k_core, k_diag)
    real, imag = (
        jnp.concatenate(
            [
                jnp.where(odd, b[part, :, mine].astype(F32), a[part, :, mine].astype(F32))
                for first, second in ((near, far), (far, near))
                for a, b in zip(first, second, strict=True)
            ],
            axis=0,
        ).T
        for part in range(2)
    )
    full = real.shape[1]
    even, odd = pl.ds(0, share, stride=2), pl.ds(1, share, stride=2)
    wide[0, even, :] = real
    wide[1, even, :] = -imag
    wide[0, odd, :] = imag
    wide[1, odd, :] = real
    folded[:, :full] = wide[0].astype(BF16)
    folded[:, full:] = wide[1].astype(BF16)


def sender(targets, cluster):
    source = jnp.int32(0)
    for at, target in enumerate(targets):
        source = jnp.where(cluster == target, at, source)
    return source


def chain_kernel(clusters, quarter, *refs):
    pieces, folded, field = refs[: 2 * clusters], refs[2 * clusters], refs[2 * clusters + 1]
    between, skeleton, kept = refs[2 * clusters + 2 :]
    row = lax.axis_index("rows")
    cluster = lax.axis_index("clus")
    block = clusters * quarter
    full = 4 * block
    for j in range(clusters):
        senders = [sender(rounds[j], cluster) for rounds in ROUNDS]
        for core in range(2):
            source = jnp.where(row % 2 == core, senders[0], senders[1])
            ref = pieces[2 * j + core]
            for at in range(2):
                first = ((row % 2) ^ core) * 2 * block + at * block
                rows = pl.ds(pl.multiple_of(first, block), block)
                for part in range(2):
                    columns = slice(part * full, (part + 1) * full)
                    skeleton[source, rows, columns] = ref[at, part].astype(F32)
                    between[source, rows, columns] = ref[at, 2 + part]

    def gather(target):
        rows = [
            skeleton[s, pl.ds(pl.multiple_of(q * block + target * quarter, quarter), quarter), :]
            for q in range(4)
            for s in range(clusters)
        ]
        return jnp.concatenate(rows, axis=0)

    def embed(target, value):
        kept[target, :full, :] = value.astype(BF16)
        kept[target, full:, :full] = (-value[:, full:]).astype(BF16)
        kept[target, full:, full:] = value[:, :full].astype(BF16)

    def own_target(source):
        blocks = []
        for q in range(4):
            rows = between[source, q * block : (q + 1) * block, :].astype(F32)
            chosen = rows[:quarter]
            for target in range(1, clusters):
                other = rows[target * quarter : (target + 1) * quarter]
                chosen = jnp.where(cluster == target, other, chosen)
            blocks.append(chosen)
        return jnp.concatenate(blocks, axis=0).astype(BF16)

    for target in range(clusters):
        embed(target, gather(target))
    for step in range(STEPS - 2):
        for source in range(clusters):
            skeleton[source] = jnp.dot(between[source], kept[source], preferred_element_type=F32)
        for target in range(clusters):
            embed(target, gather(target))
    wanted = [
        jnp.dot(own_target(source), kept[source], preferred_element_type=F32)
        for source in range(clusters)
    ]
    value = jnp.concatenate(
        [wanted[s][q * quarter : (q + 1) * quarter] for q in range(4) for s in range(clusters)], axis=0
    )
    last = jnp.concatenate([value[:, :full], value[:, full:]], axis=0).astype(BF16)
    field[...] = jnp.dot(folded[...], last, preferred_element_type=F32).astype(BF16)


def in_vmem(count):
    return [pl.BlockSpec(memory_space=pltpu.VMEM)] * count


def gather_body(excitation, leaf_factor, coupling, ranks):
    clusters, quarter, leaf = leaf_factor.shape[2:]
    share, _, angles = excitation.shape
    block = clusters * quarter
    full = 4 * block
    params = pltpu.CompilerParams(vmem_limit_bytes=32 << 20)

    def across(flip):
        return lambda v: lax.ppermute(v, "rows", [(i, i ^ flip) for i in range(4)])

    to_x, to_core = across(2), across(1)
    factor = leaf_factor.reshape(2, block, leaf)
    weights = coupling.reshape(2, block, leaf)
    l_x = to_x(factor)
    current = excitation.reshape(2 * share, angles)
    x_near = to_core(current)
    k_x = to_x(weights)
    k_core = to_core(weights)
    l_own, x_own, x_core, keep = pl.pallas_call(
        functools.partial(load_kernel, share, angles, quarter),
        out_shape=(
            jax.ShapeDtypeStruct(factor.shape, BF16),
            jax.ShapeDtypeStruct((share, 2 * angles), BF16),
            jax.ShapeDtypeStruct((share, 2 * angles), BF16),
            jax.ShapeDtypeStruct((4, block, angles), F32),
        ),
        in_specs=[pl.BlockSpec(memory_space=pltpu.SMEM)]
        + [pl.BlockSpec(memory_space=pl.ANY)] * 2
        + in_vmem(1),
        out_specs=tuple(in_vmem(4)),
        scratch_shapes=[
            pltpu.VMEM((2 * share, angles), BF16),
            pltpu.VMEM((2 * share, angles), F32),
            pltpu.SemaphoreType.DMA((2,)),
        ],
        compiler_params=params,
        name="load_own",
    )(ranks, factor, current, x_near)
    partial, kept_partial, l_all = pl.pallas_call(
        functools.partial(side_kernel, share, angles),
        out_shape=(
            jax.ShapeDtypeStruct((2, 2, block, angles), BF16),
            jax.ShapeDtypeStruct((2, 2, block, angles), F32),
            jax.ShapeDtypeStruct((4 * block, leaf), BF16),
        ),
        in_specs=in_vmem(4),
        out_specs=tuple(in_vmem(3)),
        compiler_params=params,
        cost_estimate=pl.CostEstimate(flops=1 << 30, bytes_accessed=16 << 20, transcendentals=0),
        name="side_skeleton",
    )(l_own, l_x, x_own, x_core)
    partial_x = to_x(partial)
    near = pl.pallas_call(
        near_kernel,
        out_shape=jax.ShapeDtypeStruct((2, 2 * block, 2 * block), F32),
        in_specs=in_vmem(3),
        out_specs=in_vmem(1)[0],
        scratch_shapes=[pltpu.VMEM((4 * block, leaf), BF16)],
        compiler_params=params,
        cost_estimate=pl.CostEstimate(flops=20 << 30, bytes_accessed=16 << 20, transcendentals=0),
        name="near_columns",
    )(l_all, weights, k_core)
    k_diag = to_core(k_x)
    between = pl.pallas_call(
        far_kernel,
        out_shape=jax.ShapeDtypeStruct((2, 2, block, full), BF16),
        in_specs=in_vmem(5),
        out_specs=in_vmem(1)[0],
        scratch_shapes=[pltpu.VMEM((4 * block, leaf), BF16)],
        compiler_params=params,
        name="far_columns",
    )(near, keep, l_all, k_x, k_diag)
    packed = pl.pallas_call(
        pack_kernel,
        out_shape=jax.ShapeDtypeStruct((2, 4, block, angles), BF16),
        in_specs=in_vmem(4),
        out_specs=in_vmem(1)[0],
        compiler_params=params,
        name="pack_rows",
    )(kept_partial, partial_x, keep, between)
    folded = pl.pallas_call(
        functools.partial(fold_kernel, share),
        out_shape=jax.ShapeDtypeStruct((2 * share, 2 * full), BF16),
        in_specs=in_vmem(4),
        out_specs=in_vmem(1)[0],
        scratch_shapes=[pltpu.VMEM((2, 2 * share, full), F32)],
        compiler_params=params,
        name="fold_coupling",
    )(weights, k_x, k_core, k_diag)
    held = {0: packed}
    for j in range(1, clusters):
        pairs = [
            (4 * i + row, 4 * ROUNDS[row % 2][j][i] + row) for i in range(clusters) for row in range(4)
        ]
        held[j] = lax.ppermute(packed, ("clus", "rows"), pairs)
    pieces = []
    for j in range(clusters):
        pieces += [held[j], to_core(held[j])]
    field = pl.pallas_call(
        functools.partial(chain_kernel, clusters, quarter),
        out_shape=jax.ShapeDtypeStruct((2 * share, angles), BF16),
        in_specs=in_vmem(2 * clusters + 1),
        out_specs=in_vmem(1)[0],
        scratch_shapes=[
            pltpu.VMEM((clusters, full, 2 * full), BF16),
            pltpu.VMEM((clusters, full, 2 * angles), F32),
            pltpu.VMEM((clusters, 2 * full, 2 * angles), BF16),
        ],
        compiler_params=params,
        name="skeleton_chain",
    )(*pieces, folded)
    return field.reshape(share, 2, angles)


def body(excitation, leaf_factor, coupling, ranks):
    clusters, quarter, leaf = leaf_factor.shape[2:]
    share, _, angles = excitation.shape
    rows = lax.axis_size("rows")
    full = rows * clusters * quarter
    gathered = 4 * clusters * full * (angles + full)
    fits = (
        rows == 4
        and clusters == lax.axis_size("clus")
        and clusters == len(ROUNDS[0])
        and quarter == 8
        and angles == full == 128
        and share * rows == leaf
        and gathered <= SMALL_GATHER
    )
    plan = gather_body if fits else step_body
    return plan(excitation, leaf_factor, coupling, ranks)


def solution(mesh):
    placed = (
        P(("freq", "clus", "rows"), None, None),
        P("freq", "clus", None, "rows", None),
        P("freq", "clus", None, "rows", None),
        P("freq", None),
    )
    return jax.shard_map(
        body,
        mesh=mesh,
        in_specs=placed,
        out_specs=P(("freq", "clus", "rows"), None, None),
        check_vma=False,
    )
```

```python
import functools

import jax
import jax.numpy as jnp
from jax import lax
from jax.experimental import pallas as pl
from jax.experimental.pallas import tpu as pltpu
from jax.sharding import PartitionSpec as P

STEPS = 3
F32 = jnp.float32
BF16 = jnp.bfloat16
SMALL_GATHER = 4 << 20
ROUNDS = (
    ((0, 1, 2, 3), (2, 0, 3, 1), (1, 3, 0, 2), (3, 2, 1, 0)),
    ((0, 1, 2, 3), (3, 0, 1, 2), (1, 2, 3, 0), (2, 3, 0, 1)),
)


def complex_dot(a_real, a_imag, b_real, b_imag):
    real_part = jnp.dot(a_real, b_real, preferred_element_type=F32) - jnp.dot(
        a_imag, b_imag, preferred_element_type=F32
    )
    imag_part = jnp.dot(a_real, b_imag, preferred_element_type=F32) + jnp.dot(
        a_imag, b_real, preferred_element_type=F32
    )
    return (real_part, imag_part)


def transposed_dot(columns, skel_flat):
    real_part = jnp.einsum(
        "km,kr->mr", columns[0], skel_flat[0], preferred_element_type=F32
    ) - jnp.einsum("km,kr->mr", columns[1], skel_flat[1], preferred_element_type=F32)
    imag_part = jnp.einsum(
        "km,kr->mr", columns[0], skel_flat[1], preferred_element_type=F32
    ) + jnp.einsum("km,kr->mr", columns[1], skel_flat[0], preferred_element_type=F32)
    return jnp.stack([real_part, imag_part], axis=1)


def apply_once(current, factor, weights, keep_mask, clusters, quarter, leaf_size, angles, part_row):
    gathered = lax.all_gather(current, "rows", axis=0, tiled=True)
    real_part, imag_part = complex_dot(factor[0], factor[1], gathered[:, 0], gathered[:, 1])
    skeleton = jnp.stack([real_part, imag_part]).astype(BF16).reshape(2, clusters, quarter, angles)
    received = lax.all_to_all(skeleton, "clus", split_axis=1, concat_axis=1, tiled=True)
    received = received * keep_mask[None, :, :, None]
    skel_flat = received.reshape(2, clusters * quarter, angles)
    share_rows = leaf_size // lax.axis_size("rows")
    partial_sum = transposed_dot(weights, skel_flat)
    summed = lax.psum(partial_sum, "rows")
    own_rows = lax.dynamic_slice_in_dim(summed, part_row * share_rows, share_rows, 0)
    return own_rows.astype(BF16)


def step_body(excitation, leaf_factor, coupling, ranks):
    cluster = lax.axis_index("clus")
    part_row = lax.axis_index("rows")
    clusters = leaf_factor.shape[2]
    quarter = leaf_factor.shape[3]
    leaf_size = leaf_factor.shape[4]
    angles = excitation.shape[2]
    factor = leaf_factor.reshape(2, clusters * quarter, leaf_size)
    weights = coupling.reshape(2, clusters * quarter, leaf_size)
    rank_row = lax.dynamic_slice_in_dim(ranks, cluster, 1, 0)[0]
    rank_level = part_row * quarter + jnp.arange(quarter, dtype=jnp.int32)
    keep_mask = (rank_level[None, :] < rank_row[:, None]).astype(BF16)
    current = excitation
    for step in range(STEPS):
        current = apply_once(
            current, factor, weights, keep_mask, clusters, quarter, leaf_size, angles, part_row
        )
    return current


def combine(product, rows, columns):
    real_part = product[:rows, :columns] - product[rows:, columns:]
    imag_part = product[:rows, columns:] + product[rows:, :columns]
    return real_part, imag_part


def load_kernel(
    share, angles, quarter, ranks, l_hbm, x_hbm, x_near,
    l_own, x_own, x_core, keep, x_flat, x_wide, sems,
):
    copies = [
        pltpu.make_async_copy(source, target, sems.at[i])
        for i, (source, target) in enumerate(((x_hbm, x_flat), (l_hbm, l_own)))
    ]
    for copy in copies:
        copy.start()
    row = lax.axis_index("rows")
    cluster = lax.axis_index("clus")
    level = lax.broadcasted_iota(jnp.int32, (quarter, angles), 0)
    for at, flip in enumerate((0, 2, 1, 3)):
        base = (row ^ flip) * quarter
        for target in range(keep.shape[1] // quarter):
            below = level + base < ranks[target, cluster]
            keep[at, target * quarter : (target + 1) * quarter, :] = below.astype(F32)
    copies[0].wait()
    for source, target in ((x_flat, x_own), (x_near, x_core)):
        x_wide[...] = source[...].astype(F32)
        for part in range(2):
            target[:, part * angles : (part + 1) * angles] = x_wide[
                pl.ds(part, share, stride=2), :
            ].astype(BF16)
    copies[1].wait()


def side_kernel(share, angles, l_own, l_x, x_own, x_core, keep, partial, kept_partial, l_all):
    row = lax.axis_index("rows")
    block = l_own.shape[1]
    for part in range(2):
        for at, ref in enumerate((l_own, l_x)):
            first = (2 * part + at) * block
            l_all[first : first + block, :] = ref[part]
    total = None
    for ref, quarter in ((x_own, row), (x_core, row ^ 1)):
        columns = l_all[:, pl.ds(pl.multiple_of(quarter * share, share), share)]
        term = jnp.dot(columns, ref[...], preferred_element_type=F32)
        total = term if total is None else total + term
    for part, value in enumerate(combine(total, 2 * block, angles)):
        for at in range(2):
            rows = value[at * block : (at + 1) * block] * keep[at]
            kept_partial[at, part] = rows
            partial[at, part] = rows.astype(BF16)


def operator_columns(l_all, k_refs, k_rows):
    block = k_refs[0].shape[1]
    for part in range(2):
        for at, ref in enumerate(k_refs):
            first = (2 * part + at) * block
            k_rows[first : first + block, :] = ref[part]
    product = lax.dot_general(
        l_all[...], k_rows[...], (((1,), (1,)), ((), ())), preferred_element_type=F32
    )
    return combine(product, 2 * block, 2 * block)


def near_kernel(l_all, k_own, k_core, near, k_rows):
    near[0], near[1] = operator_columns(l_all, (k_own, k_core), k_rows)


def far_kernel(near, keep, l_all, k_x, k_diag, between, k_rows):
    block = keep.shape[1]
    for part, far in enumerate(operator_columns(l_all, (k_x, k_diag), k_rows)):
        value = near[part]
        columns = [value[:, :block], far[:, :block], value[:, block:], far[:, block:]]
        value = jnp.concatenate(columns, axis=1)
        odd = lax.axis_index("rows") % 2 == 1
        value = jnp.where(odd, pltpu.roll(value, 2 * block, 1), value)
        for at in range(2):
            between[at, part] = (value[at * block : (at + 1) * block] * keep[at]).astype(BF16)


def pack_kernel(partial, partial_x, between, packed):
    for at in range(2):
        for part in range(2):
            value = partial[at, part] + partial_x[1 - at, part].astype(F32)
            packed[at, part] = value.astype(BF16)
            packed[at, 2 + part] = between[at, part]


def fold_kernel(share, k_own, k_x, k_core, k_diag, folded, wide):
    row = lax.axis_index("rows")
    mine = pl.ds(pl.multiple_of(row * share, share), share)
    odd = row % 2 == 1
    near, far = (k_own, k_x), (k_core, k_diag)
    real, imag = (
        jnp.concatenate(
            [
                jnp.where(odd, b[part, :, mine].astype(F32), a[part, :, mine].astype(F32))
                for first, second in ((near, far), (far, near))
                for a, b in zip(first, second, strict=True)
            ],
            axis=0,
        ).T
        for part in range(2)
    )
    full = real.shape[1]
    even, odd = pl.ds(0, share, stride=2), pl.ds(1, share, stride=2)
    wide[0, even, :] = real
    wide[1, even, :] = -imag
    wide[0, odd, :] = imag
    wide[1, odd, :] = real
    folded[:, :full] = wide[0].astype(BF16)
    folded[:, full:] = wide[1].astype(BF16)


def sender(targets, cluster):
    source = jnp.int32(0)
    for at, target in enumerate(targets):
        source = jnp.where(cluster == target, at, source)
    return source


def chain_kernel(clusters, quarter, *refs):
    pieces, folded, field = refs[: 2 * clusters], refs[2 * clusters], refs[2 * clusters + 1]
    between, skeleton, kept = refs[2 * clusters + 2 :]
    row = lax.axis_index("rows")
    cluster = lax.axis_index("clus")
    block = clusters * quarter
    full = 4 * block
    for j in range(clusters):
        senders = [sender(rounds[j], cluster) for rounds in ROUNDS]
        for core in range(2):
            source = jnp.where(row % 2 == core, senders[0], senders[1])
            ref = pieces[2 * j + core]
            for at in range(2):
                first = ((row % 2) ^ core) * 2 * block + at * block
                rows = pl.ds(pl.multiple_of(first, block), block)
                for part in range(2):
                    columns = slice(part * full, (part + 1) * full)
                    skeleton[source, rows, columns] = ref[at, part].astype(F32)
                    between[source, rows, columns] = ref[at, 2 + part]

    def gather(target):
        rows = [
            skeleton[s, pl.ds(pl.multiple_of(q * block + target * quarter, quarter), quarter), :]
            for q in range(4)
            for s in range(clusters)
        ]
        return jnp.concatenate(rows, axis=0)

    def embed(target, value):
        kept[target, :full, :] = value.astype(BF16)
        kept[target, full:, :full] = (-value[:, full:]).astype(BF16)
        kept[target, full:, full:] = value[:, :full].astype(BF16)

    def own_target(source):
        blocks = []
        for q in range(4):
            rows = between[source, q * block : (q + 1) * block, :].astype(F32)
            chosen = rows[:quarter]
            for target in range(1, clusters):
                other = rows[target * quarter : (target + 1) * quarter]
                chosen = jnp.where(cluster == target, other, chosen)
            blocks.append(chosen)
        return jnp.concatenate(blocks, axis=0).astype(BF16)

    for target in range(clusters):
        embed(target, gather(target))
    for step in range(STEPS - 2):
        for source in range(clusters):
            skeleton[source] = jnp.dot(between[source], kept[source], preferred_element_type=F32)
        for target in range(clusters):
            embed(target, gather(target))
    wanted = [
        jnp.dot(own_target(source), kept[source], preferred_element_type=F32)
        for source in range(clusters)
    ]
    value = jnp.concatenate(
        [wanted[s][q * quarter : (q + 1) * quarter] for q in range(4) for s in range(clusters)], axis=0
    )
    last = jnp.concatenate([value[:, :full], value[:, full:]], axis=0).astype(BF16)
    field[...] = jnp.dot(folded[...], last, preferred_element_type=F32).astype(BF16)


def in_vmem(count):
    return [pl.BlockSpec(memory_space=pltpu.VMEM)] * count


def gather_body(excitation, leaf_factor, coupling, ranks):
    clusters, quarter, leaf = leaf_factor.shape[2:]
    share, _, angles = excitation.shape
    block = clusters * quarter
    full = 4 * block
    params = pltpu.CompilerParams(vmem_limit_bytes=32 << 20)

    def across(flip):
        return lambda v: lax.ppermute(v, "rows", [(i, i ^ flip) for i in range(4)])

    to_x, to_core = across(2), across(1)
    factor = leaf_factor.reshape(2, block, leaf)
    weights = coupling.reshape(2, block, leaf)
    l_x = to_x(factor)
    current = excitation.reshape(2 * share, angles)
    x_near = to_core(current)
    to_send, _ = lax.optimization_barrier((weights, x_near))
    k_x = to_x(to_send)
    k_core = to_core(weights)
    l_own, x_own, x_core, keep = pl.pallas_call(
        functools.partial(load_kernel, share, angles, quarter),
        out_shape=(
            jax.ShapeDtypeStruct(factor.shape, BF16),
            jax.ShapeDtypeStruct((share, 2 * angles), BF16),
            jax.ShapeDtypeStruct((share, 2 * angles), BF16),
            jax.ShapeDtypeStruct((4, block, angles), F32),
        ),
        in_specs=[pl.BlockSpec(memory_space=pltpu.SMEM)]
        + [pl.BlockSpec(memory_space=pl.ANY)] * 2
        + in_vmem(1),
        out_specs=tuple(in_vmem(4)),
        scratch_shapes=[
            pltpu.VMEM((2 * share, angles), BF16),
            pltpu.VMEM((2 * share, angles), F32),
            pltpu.SemaphoreType.DMA((2,)),
        ],
        compiler_params=params,
        name="load_own",
    )(ranks, factor, current, x_near)
    partial, kept_partial, l_all = pl.pallas_call(
        functools.partial(side_kernel, share, angles),
        out_shape=(
            jax.ShapeDtypeStruct((2, 2, block, angles), BF16),
            jax.ShapeDtypeStruct((2, 2, block, angles), F32),
            jax.ShapeDtypeStruct((4 * block, leaf), BF16),
        ),
        in_specs=in_vmem(5),
        out_specs=tuple(in_vmem(3)),
        compiler_params=params,
        cost_estimate=pl.CostEstimate(flops=1 << 30, bytes_accessed=16 << 20, transcendentals=0),
        name="side_skeleton",
    )(l_own, l_x, x_own, x_core, keep)
    partial_x = to_x(partial)
    near = pl.pallas_call(
        near_kernel,
        out_shape=jax.ShapeDtypeStruct((2, 2 * block, 2 * block), F32),
        in_specs=in_vmem(3),
        out_specs=in_vmem(1)[0],
        scratch_shapes=[pltpu.VMEM((4 * block, leaf), BF16)],
        compiler_params=params,
        cost_estimate=pl.CostEstimate(flops=20 << 30, bytes_accessed=16 << 20, transcendentals=0),
        name="near_columns",
    )(l_all, weights, k_core)
    k_diag = to_core(k_x)
    between = pl.pallas_call(
        far_kernel,
        out_shape=jax.ShapeDtypeStruct((2, 2, block, full), BF16),
        in_specs=in_vmem(5),
        out_specs=in_vmem(1)[0],
        scratch_shapes=[pltpu.VMEM((4 * block, leaf), BF16)],
        compiler_params=params,
        name="far_columns",
    )(near, keep, l_all, k_x, k_diag)
    packed = pl.pallas_call(
        pack_kernel,
        out_shape=jax.ShapeDtypeStruct((2, 4, block, angles), BF16),
        in_specs=in_vmem(3),
        out_specs=in_vmem(1)[0],
        compiler_params=params,
        name="pack_rows",
    )(kept_partial, partial_x, between)
    folded = pl.pallas_call(
        functools.partial(fold_kernel, share),
        out_shape=jax.ShapeDtypeStruct((2 * share, 2 * full), BF16),
        in_specs=in_vmem(4),
        out_specs=in_vmem(1)[0],
        scratch_shapes=[pltpu.VMEM((2, 2 * share, full), F32)],
        compiler_params=params,
        name="fold_coupling",
    )(weights, k_x, k_core, k_diag)
    held = {0: packed}
    for j in range(1, clusters):
        pairs = [
            (4 * i + row, 4 * ROUNDS[row % 2][j][i] + row) for i in range(clusters) for row in range(4)
        ]
        held[j] = lax.ppermute(packed, ("clus", "rows"), pairs)
    pieces = []
    for j in range(clusters):
        pieces += [held[j], to_core(held[j])]
    field = pl.pallas_call(
        functools.partial(chain_kernel, clusters, quarter),
        out_shape=jax.ShapeDtypeStruct((2 * share, angles), BF16),
        in_specs=in_vmem(2 * clusters + 1),
        out_specs=in_vmem(1)[0],
        scratch_shapes=[
            pltpu.VMEM((clusters, full, 2 * full), BF16),
            pltpu.VMEM((clusters, full, 2 * angles), F32),
            pltpu.VMEM((clusters, 2 * full, 2 * angles), BF16),
        ],
        compiler_params=params,
        name="skeleton_chain",
    )(*pieces, folded)
    return field.reshape(share, 2, angles)


def body(excitation, leaf_factor, coupling, ranks):
    clusters, quarter, leaf = leaf_factor.shape[2:]
    share, _, angles = excitation.shape
    rows = lax.axis_size("rows")
    full = rows * clusters * quarter
    gathered = 4 * clusters * full * (angles + full)
    fits = (
        rows == 4
        and clusters == lax.axis_size("clus")
        and clusters == len(ROUNDS[0])
        and quarter == 8
        and angles == full == 128
        and share * rows == leaf
        and gathered <= SMALL_GATHER
    )
    plan = gather_body if fits else step_body
    return plan(excitation, leaf_factor, coupling, ranks)


def solution(mesh):
    placed = (
        P(("freq", "clus", "rows"), None, None),
        P("freq", "clus", None, "rows", None),
        P("freq", "clus", None, "rows", None),
        P("freq", None),
    )
    return jax.shard_map(
        body,
        mesh=mesh,
        in_specs=placed,
        out_specs=P(("freq", "clus", "rows"), None, None),
        check_vma=False,
    )
```
